128 devices in a mesh: wide: 32 (over x_lo, z, y), tp: 4 (over x_hi, core).
Axes of the slice: x: 4 (x_hi: 2, x_lo: 2; x = x_hi * 2 + x_lo), y: 4, z: 4, core: 2. Of those that a mesh axis runs over, the one named last changes fastest.
Arguments:
- cache: bfloat16 [1024, 256, 576], P('wide'), may hold values from -4 to 4
- queries: bfloat16 [32, 32, 3, 64, 576], P('wide', None, None, 'tp'), may hold values from -28 to 28
- new_latent: bfloat16 [32, 32, 3, 576], P('wide'), may hold values from -4 to 4
- cache_len: int32 [1024], replicated, may hold values from 1 to 256, 163840 in all
- owner: int32 [1024], replicated, may hold values from 0 to 31, as said below
- moe_tokens: bfloat16 [3, 1024, 7168], P(None, 'wide'), may hold values from -6 to 6
- expert_ids: int32 [3, 1024, 8], P(None, 'wide'), may hold values from 0 to 31, all different within a row; in each aligned block of 32 rows (0 to 31, 32 to 63, ..., all dimensions but the last counted through in order) at most 9 rows name the same one
- gate_weights: float32 [3, 1024, 8], P(None, 'wide'), may hold values from 0.05 to 0.5
- w_gate: bfloat16 [32, 7168, 1024], P('wide', None, 'tp'), may hold values from -0.0625 to 0.0625
- w_up: bfloat16 [32, 7168, 1024], P('wide', None, 'tp'), may hold values from -0.0625 to 0.0625
- w_down: bfloat16 [32, 1024, 7168], P('wide', 'tp'), may hold values from -0.1875 to 0.1875
Outputs:
- attn_out: bfloat16 [32, 32, 3, 64, 512], P('wide', None, None, 'tp')
- moe_out: bfloat16 [3, 1024, 7168], P(None, 'wide', 'tp')
The draws below stay inside these ranges and needn't reach their ends.
Inputs may be any that keep to these rules, and one draw needn't show every extreme that they name: Requests 32 * g to 32 * g + 31 belong to prefill group g. No decode owner serves more than 1 request of one group, and some owner serves exactly 1 from every group.
All inputs are finite; a program needn't handle non-finite values.
Results may differ from the reference program's by a relative error of at most 0.017.
Values may be sent and summed in bfloat16 or wider, within the bound.
A program may use at most 192 MiB of HBM per device.

```python
import math
import jax
import jax.numpy as jnp
import numpy as np
from jax import lax

D = 7168
HEADS = 64
KVL = 512
LAT = 576
EFF = 1024
TOPK = 8
STEPS = 3
REQ_G = 32
CTX = 256
SLICES = 4
REQ = 1024
EXPERTS = 32
PAIR = 1
CAP = 9


def latent_base(key):
    return jnp.clip(jax.random.normal(key, (REQ, CTX, LAT), jnp.float32), -4.0, 4.0)


def owner_lists(key):
    key = jax.random.fold_in(key, 23)
    groups = REQ // REQ_G
    pool = groups * PAIR
    favoured = jax.random.randint(jax.random.fold_in(key, 1), (), 0, groups)
    noise = jax.random.randint(key, (groups, pool), 0, 1 << 20)
    candidates = jnp.arange(pool, dtype=jnp.int32)
    scores = noise * pool + candidates[None, :]
    scores = jnp.where(candidates[None, :] == favoured, -1, scores)
    ordering = jnp.argsort(scores, axis=1, stable=True)[:, :REQ_G]
    return (ordering % groups).astype(jnp.int32)


def draw_cache(key, part):
    base = latent_base(key)
    return base.astype(jnp.bfloat16)


def draw_queries(key, part):
    key = jax.random.fold_in(key, 5)
    shape = (EXPERTS, EXPERTS * PAIR, STEPS, HEADS, LAT)
    values = jnp.clip(jax.random.normal(key, shape, jnp.float32), -4.0, 4.0)
    return values.astype(jnp.bfloat16)


def draw_owner(key, part):
    return owner_lists(key).reshape(REQ)


def level_of(stream_key, dims, split, low, high):
    level, own = 1.0, jax.random.fold_in(stream_key, 6)
    for position, shards_of in split:
        heights = jnp.exp(jax.random.uniform(jax.random.fold_in(own, position), (shards_of,), jnp.float32, low / len(split), high / len(split)))
        level = level * jnp.repeat(heights, dims[position] // shards_of).reshape([-1 if axis == position else 1 for axis in range(len(dims))])
    return level


def profile(amount, total, limit, slope):
    portions = [(1 << 20) // math.isqrt(standing ** slope) + 1 for standing in range(2, amount + 1)]
    spare, given = total - limit - (amount - 1), [1] * (amount - 1)
    while spare > 0:
        movable = [i for i in range(amount - 1) if given[i] < limit]
        whole, remaining = sum([portions[i] for i in movable]), spare
        for i in movable:
            more = min(limit - given[i], max(1, remaining * portions[i] // whole), spare)
            given[i] = given[i] + more
            spare = spare - more
    return np.array([limit] + given)


def ragged(rng, number_of, total, limit, slope):
    if number_of == 2:
        one = jax.random.randint(rng, (), max(1, total - limit), min(limit, total - 1) + 1)
        return jnp.stack([one, total - one])
    sizes = jnp.asarray(profile(number_of, total, limit, slope), jnp.int32)
    couples = (number_of - 1) // 2
    source_of, receiver = sizes[1:1 + 2 * couples:2], sizes[2:2 + 2 * couples:2]
    margin = jnp.minimum(source_of - 1, limit - receiver)
    moved = jax.random.randint(jax.random.fold_in(rng, 1), (couples,), 0, 1 << 20) % (margin + 1)
    sizes = sizes.at[1:1 + 2 * couples:2].set(source_of - moved).at[2:2 + 2 * couples:2].set(receiver + moved)
    return sizes[jax.random.permutation(jax.random.fold_in(rng, 2), number_of)]


def assign_block(stream_key, own, number, rows, number_of, top, limit, slope):
    sequence = jax.random.permutation(stream_key, number_of)
    crowded, ordinary = shares(number_of, rows * top, limit, slope, True), shares(number_of, rows * top, limit, slope, False)
    places = jnp.arange(number_of)

    def named(sizes, offset_by):
        used = int((sizes > 0).sum())
        fixed = max(1, used // 4)
        shifted = fixed + (places - fixed + offset_by * (used - fixed)) % max(1, number_of - fixed)
        return jnp.zeros((number_of,), jnp.int32).at[sequence[jnp.where(places < fixed, places, shifted)]].set(jnp.asarray(sizes, jnp.int32))

    sizes = jnp.where(number % 4 == 0, named(crowded, number // 4), named(ordinary, number - number // 4 - 1))
    mixed = jax.random.permutation(jax.random.fold_in(own, 3), number_of)
    giver, taker = mixed[0:number_of // 2 * 2:2], mixed[1:number_of // 2 * 2:2]
    margin = jnp.minimum(sizes[giver] - 1, limit - sizes[taker]) // 2
    margin = jnp.where((giver == sequence[0]) | (taker == sequence[0]) | (sizes[taker] == 0), 0, jnp.maximum(margin, 0))
    shifted = jax.random.randint(jax.random.fold_in(own, 4), (number_of // 2,), 0, 1 << 20) % (margin + 1)
    sizes = sizes.at[giver].add(-shifted).at[taker].add(shifted)
    items = jnp.searchsorted(jnp.cumsum(sizes), jnp.arange(rows * top), side="right").astype(jnp.int32)
    table = items.reshape(top, rows).T
    table = table[jax.random.permutation(jax.random.fold_in(own, 1), rows)]
    offset_by = jax.random.randint(jax.random.fold_in(own, 2), (rows, 1), 0, top)
    return jnp.take_along_axis(table, (jnp.arange(top)[None, :] + offset_by) % top, axis=1)


def shares(count, total, most, lean, full):
    weights = [(1 << 20) // math.isqrt(rank ** lean) + 1 for rank in range(1, count + 1)]
    largest = most if full else min(most, max(-(-total // count), total * weights[0] // sum(weights)))
    least = 1 if total - largest >= count - 1 else 0
    holding, rest = [largest] + [least] * (count - 1), total - largest - least * (count - 1)
    while rest > 0:
        free = [i for i in range(1, count) if holding[i] < largest] or [i for i in range(1, count) if holding[i] < most]
        mass, budget = sum([weights[i] for i in free]), rest
        for i in free:
            more = min(most - holding[i], max(1, budget * weights[i] // mass), rest)
            holding[i] = holding[i] + more
            rest = rest - more
    return np.array(holding)


def centred(rng, shape, width, bound, cuts=(), kind=jnp.bfloat16):
    gain = level_of(rng, shape, cuts, -0.22, 0.18) if cuts else 1.0
    entries = jax.random.normal(rng, shape, jnp.float32) * width * gain
    return jnp.minimum(jnp.maximum(entries, -bound), bound).astype(kind)


def setup_inputs(seed: int = 0) -> dict:
    key_list = jax.random.split(jax.random.key(seed), 12)
    cache = draw_cache(jax.random.fold_in(key_list[11], 71), 0)
    queries = draw_queries(jax.random.fold_in(key_list[11], 71), 0)
    new_latent = centred(key_list[2], (EXPERTS, EXPERTS * PAIR, STEPS, LAT), 1.0, 4.0, ((0, 32),))
    cache_len = ragged(key_list[3], REQ, REQ * CTX * 5 // 8, CTX, 2).astype(jnp.int32)
    owner = draw_owner(jax.random.fold_in(key_list[11], 71), 0)
    moe_tokens = centred(key_list[5], (STEPS, REQ, D), 1.0, 6.0, ((1, 32),))
    expert_ids_keys = jax.random.split(jax.random.fold_in(key_list[6], 1), STEPS * REQ // REQ_G)
    expert_ids_turns = jax.random.permutation(jax.random.fold_in(key_list[6], 3), STEPS * REQ // REQ_G)
    expert_ids = jax.vmap(lambda own, number: assign_block(jax.random.fold_in(key_list[6], 2), own, number, REQ_G, EXPERTS, TOPK, CAP, 2))(expert_ids_keys, expert_ids_turns).reshape((STEPS, REQ, TOPK))
    gate_weights = jnp.clip(0.05 + 0.45 * jax.random.uniform(key_list[7], (STEPS, REQ, TOPK), jnp.float32) ** level_of(key_list[7], (STEPS, REQ, TOPK), ((1, 32),), -0.2, 0.2), 0.05, 0.5)
    w_gate = centred(key_list[8], (EXPERTS, D, EFF), D ** -0.5, 0.0625, ((0, 32), (2, 4)))
    w_up = centred(key_list[9], (EXPERTS, D, EFF), D ** -0.5, 0.0625, ((0, 32), (2, 4)))
    w_down = centred(key_list[10], (EXPERTS, EFF, D), EFF ** -0.5, 0.1875, ((0, 32), (1, 4)))
    return {"cache": cache, "queries": queries, "new_latent": new_latent, "cache_len": cache_len, "owner": owner, "moe_tokens": moe_tokens, "expert_ids": expert_ids, "gate_weights": gate_weights, "w_gate": w_gate, "w_up": w_up, "w_down": w_down}


score_scale = 192.0 ** -0.5
masked_score = -1e30


def latent_attend(latents, queries_in, new_keys, lengths):
    lat_f = latents.astype(jnp.float32)
    qry_f = queries_in.astype(jnp.float32)
    new_f = new_keys.astype(jnp.float32)
    positions = jnp.arange(latents.shape[1], dtype=jnp.int32)
    cache_valid = (positions[None, :] < lengths[:, None])[:, None, None, :]
    step_ids = jnp.arange(queries_in.shape[1], dtype=jnp.int32)
    fresh_valid = (step_ids[None, :] <= step_ids[:, None])[None, :, None, :]
    cache_scores = jnp.einsum("gshl,gcl->gshc", qry_f, lat_f) * score_scale
    fresh_scores = jnp.einsum("gshl,gtl->gsht", qry_f, new_f) * score_scale
    cache_scores = jnp.where(cache_valid, cache_scores, masked_score)
    fresh_scores = jnp.where(fresh_valid, fresh_scores, masked_score)
    top_score = jnp.maximum(jnp.max(cache_scores, -1), jnp.max(fresh_scores, -1))[..., None]
    cache_weights = jnp.where(cache_valid, jnp.exp(cache_scores - top_score), 0.0)
    fresh_weights = jnp.where(fresh_valid, jnp.exp(fresh_scores - top_score), 0.0)
    totals = jnp.sum(cache_weights, -1) + jnp.sum(fresh_weights, -1)
    cache_round = lax.optimization_barrier(cache_weights.astype(jnp.bfloat16)).astype(jnp.float32)
    fresh_round = lax.optimization_barrier(fresh_weights.astype(jnp.bfloat16)).astype(jnp.float32)
    context = jnp.einsum("gshc,gck->gshk", cache_round, lat_f[..., :KVL])
    context = context + jnp.einsum("gsht,gtk->gshk", fresh_round, new_f[..., :KVL])
    return (context / totals[..., None]).astype(jnp.bfloat16)


def attend_group(operands):
    latents, queries_in, new_keys, lengths = operands
    return latent_attend(latents, queries_in, new_keys, lengths)


def run_expert(operands):
    rows, gate_w, up_w, down_w = operands
    gate_value = jnp.dot(rows, gate_w, preferred_element_type=jnp.float32)
    up_value = jnp.dot(rows, up_w, preferred_element_type=jnp.float32)
    hidden = (jax.nn.silu(gate_value) * up_value).astype(jnp.bfloat16)
    width_part = EFF // SLICES
    total = jnp.zeros((rows.shape[0], down_w.shape[1]), jnp.float32)
    for part_index in range(SLICES):
        low = part_index * width_part
        part_out = jnp.dot(hidden[:, low:low + width_part], down_w[low:low + width_part], preferred_element_type=jnp.float32)
        total = total + lax.optimization_barrier(part_out.astype(jnp.bfloat16)).astype(jnp.float32)
    return total.astype(jnp.bfloat16)


def reference(cache, queries, new_latent, cache_len, owner, moe_tokens, expert_ids, gate_weights, w_gate, w_up, w_down):
    groups = REQ // REQ_G
    owner_grid = owner.reshape(groups, REQ_G)
    owner_hits = (owner_grid[:, :, None] == jnp.arange(groups, dtype=jnp.int32)[None, None, :]).astype(jnp.int32)
    earlier = jnp.cumsum(owner_hits, axis=1) - owner_hits
    slot_rank = jnp.sum(earlier * owner_hits, axis=2)
    slot_index = (jnp.arange(groups, dtype=jnp.int32)[:, None] * PAIR + slot_rank).astype(jnp.int32)
    query_rows = queries[owner_grid, slot_index]
    fresh_rows = new_latent[owner_grid, slot_index]
    grouped = (cache.reshape(groups, REQ_G, CTX, LAT), query_rows, fresh_rows, cache_len.reshape(groups, REQ_G))
    contexts = lax.map(attend_group, grouped)
    attn_out = jnp.zeros((groups, groups * PAIR, STEPS, HEADS, KVL), jnp.bfloat16)
    attn_out = attn_out.at[owner_grid, slot_index].set(contexts)

    route_total = REQ_G * TOPK
    expert_range = jnp.arange(EXPERTS, dtype=jnp.int32)
    cap_range = jnp.arange(CAP, dtype=jnp.int32)
    token_of_route = (jnp.arange(route_total, dtype=jnp.int32)[:, None] // TOPK == jnp.arange(REQ_G, dtype=jnp.int32)[None, :]).astype(jnp.float32)
    outputs = []
    for decode_step in range(STEPS):
        route_ids = expert_ids[decode_step].reshape(groups, route_total)
        route_hits = (route_ids[:, :, None] == expert_range[None, None, :]).astype(jnp.int32)
        before = jnp.cumsum(route_hits, axis=1) - route_hits
        route_rank = jnp.sum(before * route_hits, axis=2)
        placed = route_hits[:, :, :, None] * (route_rank[:, :, None, None] == cap_range[None, None, None, :]).astype(jnp.int32)
        placed_f = placed.astype(jnp.float32)
        slot_tokens = jnp.einsum("nqec,qj->encj", placed_f, token_of_route)
        route_weights = gate_weights[decode_step].reshape(groups, route_total).astype(jnp.float32)
        slot_mix = jnp.einsum("nqec,qj,nq->encj", placed_f, token_of_route, route_weights)
        tokens_now = moe_tokens[decode_step].reshape(groups, REQ_G, D).astype(jnp.float32)
        slot_rows = jnp.einsum("encj,njd->encd", slot_tokens, tokens_now).astype(jnp.bfloat16)
        expert_rows = lax.map(run_expert, (slot_rows.reshape(EXPERTS, groups * CAP, D), w_gate, w_up, w_down))
        expert_rows = expert_rows.reshape(EXPERTS, groups, CAP, D).astype(jnp.float32)
        mixed_rows = jnp.einsum("encj,encd->njd", slot_mix, expert_rows)
        outputs.append(mixed_rows.reshape(REQ, D).astype(jnp.bfloat16))
    moe_out = jnp.stack(outputs)
    return attn_out, moe_out
```

```python
import jax
import jax.numpy as jnp
from jax import lax
from jax.experimental import pallas as pl
from jax.experimental.pallas import tpu as pltpu
from jax.sharding import PartitionSpec as P

MESH = pl.DeviceIdType.MESH
BF = jnp.bfloat16
F32 = jnp.float32
SCALE = 192.0 ** (-0.5)
MASKED = -1e30
HALF = 3584
QUART = 1792
CAP = 9


def offsets(j):
    a, b, far = j % 4, (j // 4) % 4, j // 16
    return (a + b + far) % 2, (a + b) % 4, a


def kernel(
    q_hbm, new_hbm, cache_hbm, tok_hbm, ids_ref, gate_ref, table, wg_hbm, wu_hbm, wd_hbm,
    attn_out, moe_out, back,
    cache_v, q_v, new_v, ctx_v, tokh_v, tokq_v, dest_v, mixw_v,
    same_v, other_v, x_v, wg_v, wu_v, wd_v, s_v, sib_v, p_v, got_v, acc_v,
    load_sem, wload_sem, wsend_sem, wrecv_sem, qsend_sem, qrecv_sem, nsend_sem, nrecv_sem,
    csend_sem, crecv_sem, dsend_sem, drecv_sem, ssend_sem, srecv_sem, psend_sem, precv_sem,
    self_sem, got_sem,
):
    w = lax.axis_index("wide")
    t = lax.axis_index("tp")
    xl, z, y = w // 16, (w // 4) % 4, w % 4
    h, c = t // 2, t % 2
    x = 2 * h + xl
    xnext, xprev = (x + 1) % 4, (x + 3) % 4
    sibling = (w, h * 2 + 1 - c)

    def wide_of(far, zz, yy):
        return ((xl + far) % 2) * 16 + ((z + zz) % 4) * 4 + (y + yy) % 4

    loads = [
        pltpu.make_async_copy(tok_hbm.at[:, pl.ds(pl.multiple_of(c * HALF, 128), HALF)], tokh_v, load_sem.at[0]),
        pltpu.make_async_copy(
            tok_hbm.at[:, pl.ds(pl.multiple_of(c * HALF + h * QUART, 128), QUART)], tokq_v, load_sem.at[1]
        ),
        pltpu.make_async_copy(cache_hbm, cache_v, load_sem.at[2]),
        pltpu.make_async_copy(q_hbm.at[w], q_v.at[0], load_sem.at[3]),
        pltpu.make_async_copy(new_hbm.at[w], new_v.at[0], load_sem.at[4]),
    ]
    for load in loads:
        load.start()
    mine = pl.ds(pl.multiple_of(c * HALF, 128), HALF)
    theirs = pl.ds(pl.multiple_of((1 - c) * HALF, 128), HALF)
    hidden_rows = pl.ds(pl.multiple_of(c * 256, 256), 256)
    wloads = [
        pltpu.make_async_copy(wg_hbm.at[mine], wg_v.at[c], wload_sem.at[0]),
        pltpu.make_async_copy(wu_hbm.at[mine], wu_v.at[c], wload_sem.at[1]),
        pltpu.make_async_copy(wd_hbm, wd_v.at[hidden_rows], wload_sem.at[2]),
    ]
    for load in wloads:
        load.start()

    barrier = pltpu.get_barrier_semaphore()

    def greet(i, carry):
        n = (w * 4 + t + i) % 128
        pl.semaphore_signal(barrier, inc=1, device_id=(n // 4, n % 4), device_id_type=MESH)
        return carry

    lax.fori_loop(1, 128, greet, 0)
    pl.semaphore_wait(barrier, 127)

    def remote(src, dst, send, recv, dev):
        return pltpu.make_async_remote_copy(
            src_ref=src, dst_ref=dst, send_sem=send, recv_sem=recv, device_id=dev, device_id_type=MESH
        )

    def send_query(j, carry):
        far, zz, yy = offsets(j)
        n = wide_of(far, zz, yy)
        remote(q_hbm.at[n], q_v.at[j], qsend_sem, qrecv_sem, (n, t)).start()
        remote(new_hbm.at[n], new_v.at[j], nsend_sem, nrecv_sem, (n, t)).start()
        return carry

    lax.fori_loop(1, 32, send_query, 0)

    swaps = [
        remote(wg_hbm.at[theirs], wg_v.at[c], wsend_sem.at[0], wrecv_sem.at[0], sibling),
        remote(wu_hbm.at[theirs], wu_v.at[c], wsend_sem.at[1], wrecv_sem.at[1], sibling),
        remote(wd_hbm, wd_v.at[hidden_rows], wsend_sem.at[2], wrecv_sem.at[2], sibling),
    ]
    for swap in swaps:
        swap.start()

    expert = lax.broadcasted_iota(jnp.int32, (32, 96), 0)
    token = lax.broadcasted_iota(jnp.int32, (32, 96), 1)
    hits = jnp.zeros((32, 96), F32)
    mixw = jnp.zeros((32, 96), F32)
    for k in range(8):
        equal = expert == ids_ref[k : k + 1, :]
        hits = jnp.where(equal, 1.0, hits)
        mixw = jnp.where(equal, gate_ref[k : k + 1, :], mixw)
    first = lax.broadcasted_iota(jnp.int32, (96, 96), 0)
    later = lax.broadcasted_iota(jnp.int32, (96, 96), 1)
    before = ((first // 32 == later // 32) & (first < later)).astype(F32)
    rank = jnp.dot(hits, before, preferred_element_type=F32)
    place = (token // 32).astype(F32) * CAP + rank
    dest_v[...] = jnp.where(hits > 0.0, place, -1.0)
    mixw_v[...] = mixw

    row_id = lax.broadcasted_iota(jnp.int32, (32, 96), 0).astype(F32)

    loads[0].wait()
    loads[1].wait()

    def send_tokens(k, carry):
        def pick(far):
            parts = []
            for a in range(4):
                e = wide_of(far, a + k, a)
                parts.append(jnp.where(row_id == dest_v[pl.ds(e, 1), :], 1.0, 0.0))
            return jnp.concatenate(parts, axis=0).astype(BF)

        base = pl.multiple_of(k * 128, 128)
        for part in range(2):
            cols = slice(part * QUART, (part + 1) * QUART)
            rows = jnp.dot(pick(0), tokh_v[:, cols], preferred_element_type=F32).astype(BF)
            same_v[pl.ds(base, 128), cols] = rows

            @pl.when(k == 0)
            def _():
                x_v[0:32, cols] = rows[0:32]

        other_v[pl.ds(base, 128), :] = jnp.dot(pick(1), tokq_v[...], preferred_element_type=F32).astype(BF)
        for rb in range(2):
            for a in range(4):
                src = pl.ds(pl.multiple_of(k * 128 + a * 32 + rb * 16, 16), 16)
                near = pl.ds(pl.multiple_of(k * 256 + a * 32 + rb * 16, 16), 16)
                away = pl.ds(pl.multiple_of(k * 256 + 128 + a * 32 + rb * 16, 16), 16)

                def send_same():
                    for part in range(2):
                        cols = pl.ds(part * QUART, QUART)
                        remote(
                            same_v.at[src, cols], x_v.at[near, cols], dsend_sem.at[0], drecv_sem.at[k],
                            (wide_of(0, a + k, a), t),
                        ).start()

                if a == 0:
                    pl.when(k > 0)(send_same)
                else:
                    send_same()
                cols = pl.ds(pl.multiple_of(h * QUART, 128), QUART)
                for i, chip in enumerate((xnext, xprev)):
                    remote(
                        other_v.at[src], x_v.at[away, cols], dsend_sem.at[1 + i], drecv_sem.at[k],
                        (wide_of(1, a + k, a), (chip // 2) * 2 + c),
                    ).start()
        return carry

    lax.fori_loop(0, 4, send_tokens, 0)

    for load in loads[2:]:
        load.wait()
    pltpu.make_async_copy(q_v.at[pl.ds(1, 31)], q_v.at[pl.ds(1, 31)], qrecv_sem).wait()
    pltpu.make_async_copy(new_v.at[pl.ds(1, 31)], new_v.at[pl.ds(1, 31)], nrecv_sem).wait()

    def attend(j, carry):
        far, zz, yy = offsets(j)
        o = wide_of(far, 4 - zz, 4 - yy)
        held = table[o]
        length = table[32 + o]
        latents = cache_v[held]
        query = q_v[j]
        packed = new_v[j]
        r16 = lax.broadcasted_iota(jnp.int32, (16, 16), 0)
        c16 = lax.broadcasted_iota(jnp.int32, (16, 16), 1)
        pieces = [
            jnp.dot(
                jnp.where((c16 == r16 * 5 + i) & (r16 < 3), 1.0, 0.0).astype(BF), packed,
                preferred_element_type=F32,
            ).astype(BF)
            for i in range(5)
        ]
        fresh_key = jnp.concatenate(pieces[:4], axis=1)
        nt = (((1,), (1,)), ((), ()))
        scores = lax.dot_general(query, latents, nt, preferred_element_type=F32) * SCALE
        fresh = lax.dot_general(query[:, :512], fresh_key, nt, preferred_element_type=F32)
        fresh += lax.dot_general(query[:, 512:], pieces[4][:, :64], nt, preferred_element_type=F32)
        fresh = fresh * SCALE
        valid = lax.broadcasted_iota(jnp.int32, (48, 256), 1) < length
        step = lax.broadcasted_iota(jnp.int32, (48, 16), 0) // 16
        fresh_valid = lax.broadcasted_iota(jnp.int32, (48, 16), 1) <= step
        scores = jnp.where(valid, scores, MASKED)
        fresh = jnp.where(fresh_valid, fresh, MASKED)
        top = jnp.maximum(
            jnp.max(scores, axis=1, keepdims=True), jnp.max(fresh, axis=1, keepdims=True)
        )
        weights = jnp.where(valid, jnp.exp(scores - top), 0.0)
        fresh_weights = jnp.where(fresh_valid, jnp.exp(fresh - top), 0.0)
        total = jnp.sum(weights, axis=1, keepdims=True) + jnp.sum(fresh_weights, axis=1, keepdims=True)
        context = jnp.dot(weights.astype(BF), latents[:, :512], preferred_element_type=F32)
        context += jnp.dot(fresh_weights.astype(BF), fresh_key, preferred_element_type=F32)
        ctx_v[j] = (context / total).astype(BF)

        @pl.when(j == 0)
        def _():
            pltpu.make_async_copy(ctx_v.at[j], attn_out.at[w], self_sem).start()

        @pl.when(j > 0)
        def _():
            remote(ctx_v.at[j], attn_out.at[w], csend_sem, crecv_sem, (o, t)).start()

        return carry

    lax.fori_loop(0, 32, attend, 0)

    for load in wloads:
        load.wait()
    for swap in swaps:
        swap.wait()

    def swap_sums(k):
        theirs = pl.ds(pl.multiple_of((1 - c) * 128, 128), 128)
        return remote(s_v.at[k, theirs], sib_v.at[k], ssend_sem.at[k], srecv_sem.at[k], sibling)

    def first_half(k):
        @pl.when(k == 0)
        def _():
            part = x_v.at[pl.ds(32, 224)]
            pltpu.make_async_copy(part, part, drecv_sem.at[k]).wait()

        @pl.when(k > 0)
        def _():
            part = x_v.at[pl.ds(pl.multiple_of(k * 256, 256), 256)]
            pltpu.make_async_copy(part, part, drecv_sem.at[k]).wait()

        rows = pl.ds(pl.multiple_of(k * 256, 256), 256)
        for core in range(2):
            for i, weight in enumerate((wg_v, wu_v)):
                col = core * 512 + i * 256
                s_v[k, :, col : col + 256] = jnp.dot(x_v[rows, :], weight[core], preferred_element_type=F32)
        swap_sums(k).start()

    def p_wait(k):
        part = p_v.at[k % 2]
        pltpu.make_async_copy(part, part, psend_sem.at[k % 2]).wait()

    def second_half(k):
        swap_sums(k).wait_recv()

        @pl.when(k >= 2)
        def _():
            p_wait(k)

        own = pl.ds(pl.multiple_of(c * 128, 128), 128)
        hidden = []
        for core in range(2):
            col = core * 512
            gate = s_v[k, own, col : col + 256] + sib_v[k, :, col : col + 256]
            up = s_v[k, own, col + 256 : col + 512] + sib_v[k, :, col + 256 : col + 512]
            hidden.append((gate / (1.0 + jnp.exp(-gate)) * up).astype(BF))
        hidden = jnp.concatenate(hidden, axis=1)
        for q in range(4):
            cols = slice(q * QUART, (q + 1) * QUART)
            p_v[k % 2, :, cols] = jnp.dot(hidden, wd_v[:, cols], preferred_element_type=F32).astype(BF)
        for q in range(4):
            for rb in range(2):
                for a in range(4):
                    n = wide_of(c, 8 - a - k, 4 - a)
                    slot = ((k * 4 + a) * 2 + c) * 2 + h
                    src = p_v.at[k % 2, pl.ds(a * 32 + rb * 16, 16), pl.ds(q * QUART, QUART)]
                    dst = back.at[slot, pl.ds(rb * 16, 16)]

                    def away():
                        remote(src, dst, psend_sem.at[k % 2], precv_sem.at[k], (n, q)).start()

                    if a > 0:
                        away()
                    else:
                        home = (k == 0) & (c == 0) & (h * 2 == q)

                        @pl.when(home)
                        def _():
                            pltpu.make_async_copy(src, dst, psend_sem.at[k % 2]).start()

                        pl.when(jnp.logical_not(home))(away)

    def expert_step(k, carry):
        @pl.when(k < 4)
        def _():
            first_half(k)

        @pl.when(k > 0)
        def _():
            second_half(k - 1)

        return carry

    lax.fori_loop(0, 5, expert_step, 0)

    acc_v[...] = jnp.zeros_like(acc_v)

    def mix(k, carry):
        @pl.when((k == 0) & (c == 0))
        def _():
            part = back.at[pl.ds(0, 15)]
            pltpu.make_async_copy(part, part, precv_sem.at[k]).wait()

        @pl.when((k > 0) | (c == 1))
        def _():
            part = back.at[pl.ds(0, 16)]
            pltpu.make_async_copy(part, part, precv_sem.at[k]).wait()

        fetch = pltpu.make_async_copy(back.at[pl.ds(k * 16, 16)], got_v, got_sem)
        fetch.start()
        parts = []
        for a in range(4):
            for far in range(2):
                e = wide_of(far, a + k, a)
                part = jnp.where(row_id == dest_v[pl.ds(e, 1), :], mixw_v[pl.ds(e, 1), :], 0.0)
                parts += [part, part]
        weights = jnp.concatenate(parts, axis=0)
        high = weights.astype(BF)
        low = (weights - high.astype(F32)).astype(BF)
        fetch.wait()
        rows = got_v[...].reshape(512, QUART)
        tn = (((0,), (0,)), ((), ()))
        acc_v[...] += lax.dot_general(high, rows, tn, preferred_element_type=F32) + lax.dot_general(
            low, rows, tn, preferred_element_type=F32
        )
        return carry

    lax.fori_loop(0, 4, mix, 0)
    moe_out[...] = acc_v[...].astype(BF)

    part = q_v.at[pl.ds(1, 31)]
    pltpu.make_async_copy(part, part, qsend_sem).wait()
    part = new_v.at[pl.ds(1, 31)]
    pltpu.make_async_copy(part, part, nsend_sem).wait()
    part = ctx_v.at[pl.ds(1, 31)]
    pltpu.make_async_copy(part, part, csend_sem).wait()
    pltpu.make_async_copy(part, part, crecv_sem).wait()
    pltpu.make_async_copy(ctx_v.at[0], attn_out.at[w], self_sem).wait()
    part = same_v.at[pl.ds(32, 480)]
    pltpu.make_async_copy(part, part, dsend_sem.at[0]).wait()
    for i in range(2):
        pltpu.make_async_copy(other_v, other_v, dsend_sem.at[1 + i]).wait()
    for k in range(4):
        swap_sums(k).wait_send()
    for k in range(2, 4):
        p_wait(k)


def shards(
    cache, queries, new_latent, cache_len, owner, moe_tokens, expert_ids, gate_weights, w_gate, w_up, w_down
):
    wide = lax.axis_index("wide")
    mine = lax.dynamic_slice_in_dim(owner, wide * 32, 32, 0)
    lengths = lax.dynamic_slice_in_dim(cache_len, wide * 32, 32, 0)
    served = mine[None, :] == jnp.arange(32, dtype=jnp.int32)[:, None]
    held = jnp.sum(jnp.where(served, jnp.arange(32, dtype=jnp.int32)[None, :], 0), axis=1)
    length = jnp.sum(jnp.where(served, lengths[None, :], 0), axis=1)
    table = jnp.concatenate([held, length])
    packed = jnp.pad(new_latent[0], ((0, 0), (0, 0), (0, 64))).reshape(32, 15, 128)
    packed = jnp.pad(packed, ((0, 0), (0, 1), (0, 0)))
    ids = expert_ids.transpose(2, 0, 1).reshape(8, 96)
    gates = gate_weights.transpose(2, 0, 1).reshape(8, 96)

    hbm = pl.BlockSpec(memory_space=pl.ANY)
    vmem = pl.BlockSpec(memory_space=pltpu.VMEM)
    dma = pltpu.SemaphoreType.DMA
    attn, moe, _ = pl.pallas_call(
        kernel,
        out_shape=(
            jax.ShapeDtypeStruct((32, 48, 512), BF),
            jax.ShapeDtypeStruct((96, QUART), BF),
            jax.ShapeDtypeStruct((64, 32, QUART), BF),
        ),
        in_specs=[hbm, hbm, hbm, hbm, vmem, vmem, pl.BlockSpec(memory_space=pltpu.SMEM), hbm, hbm, hbm],
        out_specs=(hbm, vmem, hbm),
        scratch_shapes=[
            pltpu.VMEM((32, 256, 576), BF),
            pltpu.VMEM((32, 48, 576), BF),
            pltpu.VMEM((32, 16, 128), BF),
            pltpu.VMEM((32, 48, 512), BF),
            pltpu.VMEM((96, HALF), BF),
            pltpu.VMEM((96, QUART), BF),
            pltpu.VMEM((32, 96), F32),
            pltpu.VMEM((32, 96), F32),
            pltpu.VMEM((512, HALF), BF),
            pltpu.VMEM((512, QUART), BF),
            pltpu.VMEM((1024, HALF), BF),
            pltpu.VMEM((2, HALF, 256), BF),
            pltpu.VMEM((2, HALF, 256), BF),
            pltpu.VMEM((512, 7168), BF),
            pltpu.VMEM((4, 256, 1024), F32),
            pltpu.VMEM((4, 128, 1024), F32),
            pltpu.VMEM((2, 128, 7168), BF),
            pltpu.VMEM((16, 32, QUART), BF),
            pltpu.VMEM((96, QUART), F32),
            dma((5,)), dma((3,)), dma((3,)), dma((3,)), dma, dma, dma, dma,
            dma, dma, dma((3,)), dma((4,)), dma((4,)), dma((4,)), dma((2,)), dma((4,)),
            dma, dma,
        ],
        compiler_params=pltpu.CompilerParams(
            collective_id=0, has_side_effects=True, vmem_limit_bytes=63 * 1024 * 1024
        ),
        cost_estimate=pl.CostEstimate(flops=13_000_000_000, bytes_accessed=60_000_000, transcendentals=2_000_000),
        name="handover_attend_experts",
    )(
        queries[0].reshape(32, 48, 576), packed, cache, moe_tokens.reshape(96, 7168), ids, gates, table,
        w_gate[0], w_up[0], w_down[0],
    )
    return attn.reshape(1, 32, 3, 16, 512), moe.reshape(3, 32, QUART)


def solution(mesh):
    in_specs = (
        P("wide", None, None),
        P("wide", None, None, "tp", None),
        P("wide", None, None, None),
        P(),
        P(),
        P(None, "wide", None),
        P(None, "wide", None),
        P(None, "wide", None),
        P("wide", None, "tp"),
        P("wide", None, "tp"),
        P("wide", "tp", None),
    )
    out_specs = (P("wide", None, None, "tp", None), P(None, "wide", "tp"))
    return jax.shard_map(shards, mesh=mesh, in_specs=in_specs, out_specs=out_specs, check_vma=False)
```

```python
import jax
import jax.numpy as jnp
from jax import lax
from jax.experimental import pallas as pl
from jax.experimental.pallas import tpu as pltpu
from jax.sharding import PartitionSpec as P

MESH = pl.DeviceIdType.MESH
BF = jnp.bfloat16
F32 = jnp.float32
SCALE = 192.0 ** (-0.5)
MASKED = -1e30
HALF = 3584
QUART = 1792
CAP = 9
ROWS = 27
PACK = 112


def offsets(j):
    a, b, far = j % 4, (j // 4) % 4, j // 16
    return (a + b + far) % 2, (a + b) % 4, a


def kernel(
    q_hbm, new_hbm, cache_hbm, tok_hbm, ids_ref, gate_ref, table, wg_hbm, wu_hbm, wd_hbm,
    attn_out, moe_out,
    cache_v, q_v, new_v, ctx_v, tokh_v, tokq_v, dest_v, mixw_v,
    same_v, other_v, x_v, wg_v, wu_v, wd_v, s_v, sib_v, half_v, back_v, acc_v,
    load_sem, wload_sem, wsend_sem, wrecv_sem, qsend_sem, qrecv_sem, nsend_sem, nrecv_sem,
    csend_sem, crecv_sem, dsend_sem, drecv_sem, ssend_sem, srecv_sem, psend_sem, hrecv_sem, near_sem,
    ysend_sem, yrecv_sem, self_sem,
):
    w = lax.axis_index("wide")
    t = lax.axis_index("tp")
    xl, z, y = w // 16, (w // 4) % 4, w % 4
    h, c = t // 2, t % 2
    x = 2 * h + xl
    xnext, xprev = (x + 1) % 4, (x + 3) % 4
    sibling = (w, h * 2 + 1 - c)

    def wide_of(far, zz, yy):
        return ((xl + far) % 2) * 16 + ((z + zz) % 4) * 4 + (y + yy) % 4

    loads = [
        pltpu.make_async_copy(tok_hbm.at[:, pl.ds(pl.multiple_of(c * HALF, 128), HALF)], tokh_v, load_sem.at[0]),
        pltpu.make_async_copy(
            tok_hbm.at[:, pl.ds(pl.multiple_of(c * HALF + h * QUART, 128), QUART)], tokq_v, load_sem.at[1]
        ),
        pltpu.make_async_copy(cache_hbm, cache_v, load_sem.at[2]),
        pltpu.make_async_copy(q_hbm.at[w], q_v.at[0], load_sem.at[3]),
        pltpu.make_async_copy(new_hbm.at[w], new_v.at[0], load_sem.at[4]),
    ]
    for load in loads:
        load.start()
    mine = pl.ds(pl.multiple_of(c * HALF, 128), HALF)
    theirs = pl.ds(pl.multiple_of((1 - c) * HALF, 128), HALF)
    hidden_rows = pl.ds(pl.multiple_of(c * 256, 256), 256)
    wloads = [
        pltpu.make_async_copy(wg_hbm.at[mine], wg_v.at[c], wload_sem.at[0]),
        pltpu.make_async_copy(wu_hbm.at[mine], wu_v.at[c], wload_sem.at[1]),
        pltpu.make_async_copy(wd_hbm, wd_v.at[hidden_rows], wload_sem.at[2]),
    ]
    for load in wloads:
        load.start()

    barrier = pltpu.get_barrier_semaphore()

    def greet(i, carry):
        n = (w * 4 + t + i) % 128
        pl.semaphore_signal(barrier, inc=1, device_id=(n // 4, n % 4), device_id_type=MESH)
        return carry

    lax.fori_loop(1, 128, greet, 0)

    expert = lax.broadcasted_iota(jnp.int32, (32, 96), 0)
    token = lax.broadcasted_iota(jnp.int32, (32, 96), 1)
    hits = jnp.zeros((32, 96), F32)
    mixw = jnp.zeros((32, 96), F32)
    for k in range(8):
        equal = expert == ids_ref[k : k + 1, :]
        hits = jnp.where(equal, 1.0, hits)
        mixw = jnp.where(equal, gate_ref[k : k + 1, :], mixw)
    first = lax.broadcasted_iota(jnp.int32, (96, 96), 0)
    later = lax.broadcasted_iota(jnp.int32, (96, 96), 1)
    before = ((first // 32 == later // 32) & (first < later)).astype(F32)
    rank = jnp.dot(hits, before, preferred_element_type=F32)
    place = (token // 32).astype(F32) * CAP + rank
    dest_v[...] = jnp.where(hits > 0.0, place, -1.0)
    mixw_v[...] = mixw
    row_id = lax.broadcasted_iota(jnp.int32, (32, 96), 0).astype(F32)

    packed_id = lax.broadcasted_iota(jnp.int32, (PACK, 128), 0)
    padded_id = lax.broadcasted_iota(jnp.int32, (PACK, 128), 1)
    pack = (packed_id == (padded_id // 32) * ROWS + padded_id % 32) & (padded_id % 32 < ROWS)
    pack = jnp.where(pack, 1.0, 0.0).astype(BF)

    pl.semaphore_wait(barrier, 127)

    def remote(src, dst, send, recv, dev):
        return pltpu.make_async_remote_copy(
            src_ref=src, dst_ref=dst, send_sem=send, recv_sem=recv, device_id=dev, device_id_type=MESH
        )

    def send_tokens(k):
        def pick(far):
            parts = []
            for a in range(4):
                e = wide_of(far, a + k, a)
                parts.append(jnp.where(row_id == dest_v[pl.ds(e, 1), :], 1.0, 0.0))
            return jnp.concatenate(parts, axis=0).astype(BF)

        picked = pick(0)
        for part in range(2):
            rows = jnp.dot(
                picked, tokh_v[:, part * QUART : (part + 1) * QUART], preferred_element_type=F32
            ).astype(BF)
            for i in range(7):
                same_v[k, part * 7 + i] = rows[:, i * 256 : (i + 1) * 256]

        @pl.when(k == 0)
        def _():
            for i in range(14):
                x_v[0, i, 0:32, :] = same_v[0, i, 0:32, :]

        rows = jnp.dot(pick(1), tokq_v[...], preferred_element_type=F32).astype(BF)
        for i in range(7):
            other_v[k, i] = rows[:, i * 256 : (i + 1) * 256]
        for low, many in ((0, 4), (4, 3)):
            for a in range(4):
                src = pl.ds(a * 32, 32)
                away = pl.ds(128 + a * 32, 32)

                def send_same():
                    for part in range(2):
                        blocks = pl.ds(part * 7 + low, many)
                        remote(
                            same_v.at[k, blocks, src], x_v.at[k, blocks, src], dsend_sem.at[0], drecv_sem.at[k],
                            (wide_of(0, a + k, a), t),
                        ).start()

                if a == 0:
                    pl.when(k > 0)(send_same)
                else:
                    send_same()
                for i, chip in enumerate((xnext, xprev)):
                    remote(
                        other_v.at[k, pl.ds(low, many), src], x_v.at[k, pl.ds(h * 7 + low, many), away],
                        dsend_sem.at[1 + i], drecv_sem.at[k],
                        (wide_of(1, a + k, a), (chip // 2) * 2 + c),
                    ).start()

    loads[0].wait()
    loads[1].wait()
    send_tokens(0)

    swaps = [
        remote(wg_hbm.at[theirs], wg_v.at[c], wsend_sem.at[0], wrecv_sem.at[0], sibling),
        remote(wu_hbm.at[theirs], wu_v.at[c], wsend_sem.at[1], wrecv_sem.at[1], sibling),
        remote(wd_hbm, wd_v.at[hidden_rows], wsend_sem.at[2], wrecv_sem.at[2], sibling),
    ]
    for swap in swaps:
        swap.start()

    def send_query(j, carry):
        far, zz, yy = offsets(j)
        n = wide_of(far, zz, yy)
        remote(q_hbm.at[n], q_v.at[j], qsend_sem, qrecv_sem, (n, t)).start()
        remote(new_hbm.at[n], new_v.at[j], nsend_sem, nrecv_sem, (n, t)).start()
        return carry

    lax.fori_loop(1, 32, send_query, 0)
    send_tokens(1)

    for load in loads[2:]:
        load.wait()
    for load in wloads:
        load.wait()
    for swap in swaps:
        swap.wait()

    def attend(j, carry):
        far, zz, yy = offsets(j)
        o = wide_of(far, 4 - zz, 4 - yy)
        held = table[o]
        length = table[32 + o]
        latents = cache_v[held]
        query = q_v[j]
        packed = new_v[j]
        r16 = lax.broadcasted_iota(jnp.int32, (16, 16), 0)
        c16 = lax.broadcasted_iota(jnp.int32, (16, 16), 1)
        pieces = [
            jnp.dot(
                jnp.where((c16 == r16 * 5 + i) & (r16 < 3), 1.0, 0.0).astype(BF), packed,
                preferred_element_type=F32,
            ).astype(BF)
            for i in range(5)
        ]
        fresh_key = jnp.concatenate(pieces[:4], axis=1)
        nt = (((1,), (1,)), ((), ()))
        scores = jnp.dot(query, latents, preferred_element_type=F32) * SCALE
        fresh = lax.dot_general(query[:, :512], fresh_key, nt, preferred_element_type=F32)
        fresh += lax.dot_general(query[:, 512:], pieces[4][:, :64], nt, preferred_element_type=F32)
        fresh = fresh * SCALE
        valid = lax.broadcasted_iota(jnp.int32, (48, 256), 1) < length
        step = lax.broadcasted_iota(jnp.int32, (48, 16), 0) // 16
        fresh_valid = lax.broadcasted_iota(jnp.int32, (48, 16), 1) <= step
        scores = jnp.where(valid, scores, MASKED)
        fresh = jnp.where(fresh_valid, fresh, MASKED)
        top = jnp.maximum(
            jnp.max(scores, axis=1, keepdims=True), jnp.max(fresh, axis=1, keepdims=True)
        )
        weights = jnp.where(valid, jnp.exp(scores - top), 0.0)
        fresh_weights = jnp.where(fresh_valid, jnp.exp(fresh - top), 0.0)
        total = jnp.sum(weights, axis=1, keepdims=True) + jnp.sum(fresh_weights, axis=1, keepdims=True)
        context = lax.dot_general(weights.astype(BF), latents[:512, :], nt, preferred_element_type=F32)
        context += jnp.dot(fresh_weights.astype(BF), fresh_key, preferred_element_type=F32)
        ctx_v[j] = (context / total).astype(BF)

        @pl.when(j == 0)
        def _():
            pltpu.make_async_copy(ctx_v.at[j], attn_out.at[w], self_sem).start()

        @pl.when(j > 0)
        def _():
            remote(ctx_v.at[j], attn_out.at[w], csend_sem, crecv_sem, (o, t)).start()

        return carry

    def swap_sums(k):
        theirs = pl.ds(pl.multiple_of((1 - c) * 128, 128), 128)
        return remote(s_v.at[k, theirs], sib_v.at[k], ssend_sem.at[k], srecv_sem.at[k], sibling)

    def gate_and_up(k):
        @pl.when(k == 0)
        def _():
            part = x_v.at[k, :, pl.ds(32, 224)]
            pltpu.make_async_copy(part, part, drecv_sem.at[k]).wait()

        @pl.when(k > 0)
        def _():
            part = x_v.at[k]
            pltpu.make_async_copy(part, part, drecv_sem.at[k]).wait()

        rows = jnp.concatenate([x_v[k, i] for i in range(14)], axis=1)
        for core in range(2):
            for i, weight in enumerate((wg_v, wu_v)):
                col = core * 512 + i * 256
                s_v[k, :, col : col + 256] = jnp.dot(rows, weight[core], preferred_element_type=F32)
        swap_sums(k).start()

    def down(k):
        swap_sums(k).wait_recv()
        own = pl.ds(pl.multiple_of(c * 128, 128), 128)
        hidden = []
        for core in range(2):
            col = core * 512
            gate = s_v[k, own, col : col + 256] + sib_v[k, :, col : col + 256]
            up = s_v[k, own, col + 256 : col + 512] + sib_v[k, :, col + 256 : col + 512]
            hidden.append((gate / (1.0 + jnp.exp(-gate)) * up).astype(BF))
        hidden = jnp.concatenate(hidden, axis=1)
        hidden = jnp.dot(pack, hidden, preferred_element_type=F32).astype(BF)
        for i in range(28):
            x_v[k, i % 14, (i // 14) * 128 : (i // 14) * 128 + PACK, :] = jnp.dot(
                hidden, wd_v[:, i * 256 : (i + 1) * 256], preferred_element_type=F32
            ).astype(BF)

        def block(tq, i):
            n = tq * 7 + i
            return x_v.at[k, n % 14, pl.ds(pl.multiple_of((n // 14) * 128, 128), PACK)]

        @pl.when(c == 0)
        def _():
            for i in range(7):
                for core in range(2):
                    tq = 2 * (1 - h) + core
                    remote(
                        block(tq, i), half_v.at[k, 1, i], psend_sem.at[k], hrecv_sem.at[k], (w, tq)
                    ).start()
                pltpu.make_async_copy(block(2 * h, i), half_v.at[k, 0, i], psend_sem.at[k]).start()
                remote(
                    block(2 * h + 1, i), half_v.at[k, 0, i], psend_sem.at[k], near_sem.at[k], sibling
                ).start()

        @pl.when(c == 1)
        def _():
            for i in range(7):
                for tq in (0, 2, 1, 3):
                    remote(
                        block(tq, i), half_v.at[k, 2 + h, i], psend_sem.at[k], hrecv_sem.at[k],
                        (wide_of(1, 0, 0), tq),
                    ).start()

    def finish(k):
        part = x_v.at[k, :, pl.ds(0, 2 * PACK)]
        pltpu.make_async_copy(part, part, psend_sem.at[k]).wait()
        part = half_v.at[k, pl.ds(1, 3)]
        pltpu.make_async_copy(part, part, hrecv_sem.at[k]).wait()

        @pl.when(c == 1)
        def _():
            part = half_v.at[k, 0]
            pltpu.make_async_copy(part, part, near_sem.at[k]).wait()

        tn = (((0,), (0,)), ((), ()))
        for far in range(2):
            for i in range(7):
                both = half_v[k, 2 * far, i].astype(F32) + half_v[k, 2 * far + 1, i].astype(F32)
                x_v[k, far * 7 + i, 0:128, :] = lax.dot_general(
                    pack, both.astype(BF), tn, preferred_element_type=F32
                ).astype(BF)
        for low, many in ((0, 4), (4, 3), (7, 4), (11, 3)):
            for a in range(4):
                n = wide_of(0, 8 - a - k, 4 - a)
                src = x_v.at[k, pl.ds(low, many), pl.ds(a * 32, 32)]
                dst = back_v.at[k * 4 + a, pl.ds(low, many)]

                def away():
                    remote(src, dst, ysend_sem.at[k], yrecv_sem.at[k], (n, t)).start()

                if a > 0:
                    away()
                else:
                    @pl.when(k == 0)
                    def _():
                        pltpu.make_async_copy(src, dst, ysend_sem.at[k]).start()

                    pl.when(k > 0)(away)

    def expert_step(k, carry):
        @pl.when(k < 4)
        def _():
            gate_and_up(k)

        @pl.when(k < 2)
        def _():
            send_tokens(k + 2)

        @pl.when(k < 4)
        def _():
            down(k)

        @pl.when(k == 0)
        def _():
            part = q_v.at[pl.ds(1, 31)]
            pltpu.make_async_copy(part, part, qrecv_sem).wait()
            part = new_v.at[pl.ds(1, 31)]
            pltpu.make_async_copy(part, part, nrecv_sem).wait()

        @pl.when(k > 0)
        def _():
            finish(k - 1)

        @pl.when(k < 4)
        def _():
            lax.fori_loop(k * 8, k * 8 + 8, attend, 0)

        return carry

    lax.fori_loop(0, 5, expert_step, 0)

    acc_v[...] = jnp.zeros_like(acc_v)

    def mix(k, carry):
        part = x_v.at[k, :, pl.ds(0, 128)]
        pltpu.make_async_copy(part, part, ysend_sem.at[k]).wait()

        @pl.when(k == 0)
        def _():
            part = back_v.at[pl.ds(1, 3)]
            pltpu.make_async_copy(part, part, yrecv_sem.at[k]).wait()

        @pl.when(k > 0)
        def _():
            part = back_v.at[pl.ds(k * 4, 4)]
            pltpu.make_async_copy(part, part, yrecv_sem.at[k]).wait()

        parts = []
        for far in range(2):
            for a in range(4):
                e = wide_of(far, a + k, a)
                parts.append(jnp.where(row_id == dest_v[pl.ds(e, 1), :], mixw_v[pl.ds(e, 1), :], 0.0))
        weights = jnp.concatenate(parts, axis=0)
        high = weights.astype(BF)
        low = (weights - high.astype(F32)).astype(BF)
        tn = (((0,), (0,)), ((), ()))
        for i in range(7):
            rows = jnp.concatenate([back_v[k * 4 + a, far * 7 + i] for far in range(2) for a in range(4)], axis=0)
            acc_v[:, i * 256 : (i + 1) * 256] += lax.dot_general(
                high, rows, tn, preferred_element_type=F32
            ) + lax.dot_general(low, rows, tn, preferred_element_type=F32)
        return carry

    lax.fori_loop(0, 4, mix, 0)
    moe_out[...] = acc_v[...].astype(BF)

    part = q_v.at[pl.ds(1, 31)]
    pltpu.make_async_copy(part, part, qsend_sem).wait()
    part = new_v.at[pl.ds(1, 31)]
    pltpu.make_async_copy(part, part, nsend_sem).wait()
    part = ctx_v.at[pl.ds(1, 31)]
    pltpu.make_async_copy(part, part, csend_sem).wait()
    pltpu.make_async_copy(part, part, crecv_sem).wait()
    pltpu.make_async_copy(ctx_v.at[0], attn_out.at[w], self_sem).wait()
    part = x_v.at[pl.ds(0, 3), :, pl.ds(0, 160)]
    pltpu.make_async_copy(part, part, dsend_sem.at[0]).wait()
    for i in range(2):
        pltpu.make_async_copy(other_v, other_v, dsend_sem.at[1 + i]).wait()
    for k in range(4):
        swap_sums(k).wait_send()


def shards(
    cache, queries, new_latent, cache_len, owner, moe_tokens, expert_ids, gate_weights, w_gate, w_up, w_down
):
    wide = lax.axis_index("wide")
    mine = lax.dynamic_slice_in_dim(owner, wide * 32, 32, 0)
    lengths = lax.dynamic_slice_in_dim(cache_len, wide * 32, 32, 0)
    served = mine[None, :] == jnp.arange(32, dtype=jnp.int32)[:, None]
    held = jnp.sum(jnp.where(served, jnp.arange(32, dtype=jnp.int32)[None, :], 0), axis=1)
    length = jnp.sum(jnp.where(served, lengths[None, :], 0), axis=1)
    table = jnp.concatenate([held, length])
    packed = jnp.pad(new_latent[0], ((0, 0), (0, 0), (0, 64))).reshape(32, 15, 128)
    packed = jnp.pad(packed, ((0, 0), (0, 1), (0, 0)))
    ids = expert_ids.transpose(2, 0, 1).reshape(8, 96)
    gates = gate_weights.transpose(2, 0, 1).reshape(8, 96)

    hbm = pl.BlockSpec(memory_space=pl.ANY)
    vmem = pl.BlockSpec(memory_space=pltpu.VMEM)
    dma = pltpu.SemaphoreType.DMA
    attn, moe = pl.pallas_call(
        kernel,
        out_shape=(
            jax.ShapeDtypeStruct((32, 48, 512), BF),
            jax.ShapeDtypeStruct((96, QUART), BF),
        ),
        in_specs=[hbm, hbm, hbm, hbm, vmem, vmem, pl.BlockSpec(memory_space=pltpu.SMEM), hbm, hbm, hbm],
        out_specs=(hbm, vmem),
        scratch_shapes=[
            pltpu.VMEM((32, 576, 256), BF),
            pltpu.VMEM((32, 48, 576), BF),
            pltpu.VMEM((32, 16, 128), BF),
            pltpu.VMEM((32, 48, 512), BF),
            pltpu.VMEM((96, HALF), BF),
            pltpu.VMEM((96, QUART), BF),
            pltpu.VMEM((32, 96), F32),
            pltpu.VMEM((32, 96), F32),
            pltpu.VMEM((4, 14, 128, 256), BF),
            pltpu.VMEM((4, 7, 128, 256), BF),
            pltpu.VMEM((4, 14, 256, 256), BF),
            pltpu.VMEM((2, HALF, 256), BF),
            pltpu.VMEM((2, HALF, 256), BF),
            pltpu.VMEM((512, 7168), BF),
            pltpu.VMEM((4, 256, 1024), F32),
            pltpu.VMEM((4, 128, 1024), F32),
            pltpu.VMEM((4, 4, 7, PACK, 256), BF),
            pltpu.VMEM((16, 14, 32, 256), BF),
            pltpu.VMEM((96, QUART), F32),
            dma((5,)), dma((3,)), dma((3,)), dma((3,)), dma, dma, dma, dma,
            dma, dma, dma((3,)), dma((4,)), dma((4,)), dma((4,)), dma((4,)), dma((4,)), dma((4,)),
            dma((4,)), dma((4,)), dma,
        ],
        compiler_params=pltpu.CompilerParams(
            collective_id=0, has_side_effects=True, vmem_limit_bytes=63 * 1024 * 1024
        ),
        cost_estimate=pl.CostEstimate(flops=13_000_000_000, bytes_accessed=60_000_000, transcendentals=2_000_000),
        name="handover_attend_experts",
    )(
        queries[0].reshape(32, 48, 576), packed, cache.transpose(0, 2, 1), moe_tokens.reshape(96, 7168), ids, gates, table,
        w_gate[0], w_up[0], w_down[0],
    )
    return attn.reshape(1, 32, 3, 16, 512), moe.reshape(3, 32, QUART)


def solution(mesh):
    in_specs = (
        P("wide", None, None),
        P("wide", None, None, "tp", None),
        P("wide", None, None, None),
        P(),
        P(),
        P(None, "wide", None),
        P(None, "wide", None),
        P(None, "wide", None),
        P("wide", None, "tp"),
        P("wide", None, "tp"),
        P("wide", "tp", None),
    )
    out_specs = (P("wide", None, None, "tp", None), P(None, "wide", "tp"))
    return jax.shard_map(shards, mesh=mesh, in_specs=in_specs, out_specs=out_specs, check_vma=False)
```

```python
import jax
import jax.numpy as jnp
from jax import lax
from jax.experimental import pallas as pl
from jax.experimental.pallas import tpu as pltpu
from jax.sharding import PartitionSpec as P

MESH = pl.DeviceIdType.MESH
BF = jnp.bfloat16
F32 = jnp.float32
SCALE = 192.0 ** (-0.5)
MASKED = -1e30
HALF = 3584
QUART = 1792
CAP = 9
ROWS = 27
PACK = 112


def offsets(j):
    a, b, far = j % 4, (j // 4) % 4, j // 16
    return (a + b + far) % 2, (a + b) % 4, a


def kernel(
    q_hbm, new_hbm, cache_hbm, tok_hbm, ids_ref, gate_ref, owner_ref, length_ref, wg_hbm, wu_hbm, wd_hbm,
    attn_out, moe_out,
    cache_v, q_v, new_v, ctx_v, tok_v, dest_v, mixw_v, near_v, picks_v,
    same_v, other_v, x_v, wg_v, wu_v, wd_v, s_v, sib_v, half_v, back_v, acc_v,
    load_sem, wload_sem, wsend_sem, wrecv_sem, qsend_sem, qrecv_sem, nsend_sem, nrecv_sem,
    csend_sem, crecv_sem, gsend_sem, grecv_sem, tsend_sem, trecv_sem, dsend_sem, drecv_sem, ssend_sem, srecv_sem, psend_sem, hrecv_sem, near_sem,
    ysend_sem, yrecv_sem, self_sem,
):
    w = lax.axis_index("wide")
    t = lax.axis_index("tp")
    xl, z, y = w // 16, (w // 4) % 4, w % 4
    h, c = t // 2, t % 2
    sibling = (w, h * 2 + 1 - c)

    def wide_of(far, zz, yy):
        return ((xl + far) % 2) * 16 + ((z + zz) % 4) * 4 + (y + yy) % 4

    mine = pl.ds(pl.multiple_of(c * HALF, 128), HALF)
    theirs = pl.ds(pl.multiple_of((1 - c) * HALF, 128), HALF)
    loads = [
        pltpu.make_async_copy(tok_hbm.at[:, mine], tok_v.at[pl.ds(0, 96)], load_sem.at[0]),
        pltpu.make_async_copy(cache_hbm, cache_v, load_sem.at[1]),
        pltpu.make_async_copy(q_hbm.at[w], q_v.at[0], load_sem.at[2]),
        pltpu.make_async_copy(new_hbm.at[w], new_v.at[0], load_sem.at[3]),
    ]
    for load in loads:
        load.start()
    hidden_rows = pl.ds(pl.multiple_of(c * 256, 256), 256)
    wloads = [
        pltpu.make_async_copy(wg_hbm.at[mine], wg_v.at[c], wload_sem.at[0]),
        pltpu.make_async_copy(wu_hbm.at[mine], wu_v.at[c], wload_sem.at[1]),
        pltpu.make_async_copy(wd_hbm, wd_v.at[hidden_rows], wload_sem.at[2]),
    ]
    for load in wloads:
        load.start()

    barrier = pltpu.get_barrier_semaphore()

    def greet(n, tq):
        pl.semaphore_signal(barrier, inc=1, device_id=(n, tq), device_id_type=MESH)

    def greet_wide(i, carry):
        greet((w + i) % 32, t)
        return carry

    lax.fori_loop(1, 32, greet_wide, 0)
    for i in range(4):
        greet(wide_of(1, i, 0), (1 - h) * 2 + c)
    for i in range(1, 4):
        greet(wide_of(1, 0, i), (1 - h) * 2 + c)
        greet(w, (t + i) % 4)
    for i in range(2):
        greet(wide_of(1, 0, 0), i * 2 + 1 - c)

    expert = lax.broadcasted_iota(jnp.int32, (32, 96), 0)
    token = lax.broadcasted_iota(jnp.int32, (32, 96), 1)
    hits = jnp.zeros((32, 96), F32)
    mixw = jnp.zeros((32, 96), F32)
    ids = jnp.concatenate([ids_ref[i] for i in range(3)], axis=1)
    gates = jnp.concatenate([gate_ref[i] for i in range(3)], axis=1)
    for k in range(8):
        equal = expert == ids[k : k + 1, :]
        hits = jnp.where(equal, 1.0, hits)
        mixw = jnp.where(equal, gates[k : k + 1, :], mixw)
    first = lax.broadcasted_iota(jnp.int32, (96, 96), 0)
    later = lax.broadcasted_iota(jnp.int32, (96, 96), 1)
    before = ((first // 32 == later // 32) & (first < later)).astype(F32)
    rank = jnp.dot(hits, before, preferred_element_type=F32)
    place = (token // 32).astype(F32) * CAP + rank
    dest_v[...] = jnp.where(hits > 0.0, place, -1.0)
    near_v[0] = dest_v[...]
    mixw_v[...] = mixw
    row_id = lax.broadcasted_iota(jnp.int32, (32, 96), 0).astype(F32)

    packed_id = lax.broadcasted_iota(jnp.int32, (PACK, 128), 0)
    padded_id = lax.broadcasted_iota(jnp.int32, (PACK, 128), 1)
    pack = (packed_id == (padded_id // 32) * ROWS + padded_id % 32) & (padded_id % 32 < ROWS)
    pack = jnp.where(pack, 1.0, 0.0).astype(BF)

    pl.semaphore_wait(barrier, 43)

    def remote(src, dst, send, recv, dev):
        return pltpu.make_async_remote_copy(
            src_ref=src, dst_ref=dst, send_sem=send, recv_sem=recv, device_id=dev, device_id_type=MESH
        )

    for d in range(1, 4):
        peer = (wide_of(0, (1 - c) * d, c * d), t)
        remote(near_v.at[0], near_v.at[d], tsend_sem, trecv_sem, peer).start()
    for part in range(4):
        for d in range(1, 4):
            peer = (wide_of(0, (1 - c) * d, c * d), t)
            cols = pl.ds(part * 896, 896)
            remote(
                tok_hbm.at[:, pl.ds(pl.multiple_of(c * HALF + part * 896, 128), 896)],
                tok_v.at[pl.ds(d * 96, 96), cols], gsend_sem, grecv_sem, peer,
            ).start()

    def send_tokens(k):
        def pick(far):
            parts = []
            for a in range(4):
                e = wide_of(far, c * (a + k), (1 - c) * a)
                held = (a + (1 - c) * k) % 4
                rows = lax.broadcasted_iota(jnp.int32, (32, 384), 0).astype(F32)
                group = lax.broadcasted_iota(jnp.int32, (32, 384), 1) // 96
                chosen = (rows == picks_v[pl.ds(e, 1), :]) & (group == held)
                parts.append(jnp.where(chosen, 1.0, 0.0))
            return jnp.concatenate(parts, axis=0).astype(BF)

        for far, out in ((0, same_v), (1, other_v)):
            picked = pick(far)
            for part in range(2):
                rows = jnp.dot(
                    picked, tok_v[:, part * QUART : (part + 1) * QUART], preferred_element_type=F32
                ).astype(BF)
                for i in range(7):
                    out[k, part * 7 + i] = rows[:, i * 256 : (i + 1) * 256]

        home = c * ((4 - k) % 4)
        kept = pl.ds(pl.multiple_of(home * 32, 32), 32)
        for i in range(14):
            x_v[k, i, kept, :] = same_v[k, i, kept, :]
        for piece in range(5):
            low, many = piece * 3, 3 if piece < 4 else 2
            far_low, far_many = ((0, 3), (3, 2), (5, 3), (8, 3), (11, 3))[piece]
            far_chip = t if piece < 2 else (1 - h) * 2 + c
            for a in range(4):
                src = pl.ds(a * 32, 32)
                away = pl.ds(128 + a * 32, 32)

                @pl.when(home != a)
                def _():
                    blocks = pl.ds(low, many)
                    remote(
                        same_v.at[k, blocks, src], x_v.at[k, blocks, src], dsend_sem.at[0], drecv_sem.at[k],
                        (wide_of(0, c * (a + k), (1 - c) * a), t),
                    ).start()

                blocks = pl.ds(far_low, far_many)
                remote(
                    other_v.at[k, blocks, src], x_v.at[k, blocks, away], dsend_sem.at[1], drecv_sem.at[k],
                    (wide_of(1, c * (a + k), (1 - c) * a), far_chip),
                ).start()

    swaps = [
        remote(wg_hbm.at[theirs], wg_v.at[c], wsend_sem.at[0], wrecv_sem.at[0], sibling),
        remote(wu_hbm.at[theirs], wu_v.at[c], wsend_sem.at[1], wrecv_sem.at[1], sibling),
        remote(wd_hbm, wd_v.at[hidden_rows], wsend_sem.at[2], wrecv_sem.at[2], sibling),
    ]
    for swap in swaps:
        swap.start()

    def send_query(j, carry):
        far, zz, yy = offsets(j)
        n = wide_of(far, zz, yy)
        remote(q_hbm.at[n], q_v.at[j], qsend_sem, qrecv_sem, (n, t)).start()
        remote(new_hbm.at[n], new_v.at[j], nsend_sem, nrecv_sem, (n, t)).start()
        return carry

    lax.fori_loop(1, 16, send_query, 0)
    loads[0].wait()
    part = near_v.at[pl.ds(1, 3)]
    pltpu.make_async_copy(part, part, trecv_sem).wait()
    part = tok_v.at[pl.ds(96, 288)]
    pltpu.make_async_copy(part, part, grecv_sem).wait()
    picks_v[...] = jnp.concatenate([near_v[i] for i in range(4)], axis=1)
    send_tokens(0)
    lax.fori_loop(16, 32, send_query, 0)
    send_tokens(1)

    for load in loads[1:]:
        load.wait()
    for load in wloads:
        load.wait()
    for swap in swaps:
        swap.wait()

    def attend(j, carry):
        far, zz, yy = offsets(j)
        o = wide_of(far, 4 - zz, 4 - yy)

        def find(r, found):
            return jnp.where(owner_ref[w * 32 + r] == o, r, found)

        held = lax.fori_loop(0, 32, find, 0)
        length = length_ref[w * 32 + held]
        latents = cache_v[held]
        query = q_v[j]
        packed = new_v[j]
        r16 = lax.broadcasted_iota(jnp.int32, (16, 16), 0)
        c16 = lax.broadcasted_iota(jnp.int32, (16, 16), 1)
        pieces = [
            jnp.dot(
                jnp.where((c16 == r16 * 5 + i) & (r16 < 3), 1.0, 0.0).astype(BF), packed,
                preferred_element_type=F32,
            ).astype(BF)
            for i in range(5)
        ]
        fresh_key = jnp.concatenate(pieces[:4], axis=1)
        nt = (((1,), (1,)), ((), ()))
        scores = jnp.dot(query, latents, preferred_element_type=F32) * SCALE
        fresh = lax.dot_general(query[:, :512], fresh_key, nt, preferred_element_type=F32)
        fresh += lax.dot_general(query[:, 512:], pieces[4][:, :64], nt, preferred_element_type=F32)
        fresh = fresh * SCALE
        valid = lax.broadcasted_iota(jnp.int32, (48, 256), 1) < length
        step = lax.broadcasted_iota(jnp.int32, (48, 16), 0) // 16
        fresh_valid = lax.broadcasted_iota(jnp.int32, (48, 16), 1) <= step
        scores = jnp.where(valid, scores, MASKED)
        fresh = jnp.where(fresh_valid, fresh, MASKED)
        top = jnp.maximum(
            jnp.max(scores, axis=1, keepdims=True), jnp.max(fresh, axis=1, keepdims=True)
        )
        weights = jnp.where(valid, jnp.exp(scores - top), 0.0)
        fresh_weights = jnp.where(fresh_valid, jnp.exp(fresh - top), 0.0)
        total = jnp.sum(weights, axis=1, keepdims=True) + jnp.sum(fresh_weights, axis=1, keepdims=True)
        context = lax.dot_general(weights.astype(BF), latents[:512, :], nt, preferred_element_type=F32)
        context += jnp.dot(fresh_weights.astype(BF), fresh_key, preferred_element_type=F32)
        ctx_v[j] = (context / total).astype(BF)

        @pl.when(j == 0)
        def _():
            pltpu.make_async_copy(ctx_v.at[j], attn_out.at[w], self_sem).start()

        @pl.when(j > 0)
        def _():
            remote(ctx_v.at[j], attn_out.at[w], csend_sem, crecv_sem, (o, t)).start()

        return carry

    def swap_sums(k):
        theirs = pl.ds(pl.multiple_of((1 - c) * 128, 128), 128)
        return remote(s_v.at[k % 2, theirs], sib_v.at[k], ssend_sem.at[k % 2], srecv_sem.at[k], sibling)

    def gate_and_up(k):
        part = x_v.at[k, :, pl.ds(0, 224)]
        pltpu.make_async_copy(part, part, drecv_sem.at[k]).wait()

        @pl.when(k >= 2)
        def _():
            swap_sums(k).wait_send()

        rows = jnp.concatenate([x_v[k, i] for i in range(14)], axis=1)
        for core in range(2):
            for i, weight in enumerate((wg_v, wu_v)):
                col = core * 512 + i * 256
                s_v[k % 2, :, col : col + 256] = jnp.dot(rows, weight[core], preferred_element_type=F32)
        swap_sums(k).start()

    def down(k):
        swap_sums(k).wait_recv()
        own = pl.ds(pl.multiple_of(c * 128, 128), 128)
        hidden = []
        for core in range(2):
            col = core * 512
            gate = s_v[k % 2, own, col : col + 256] + sib_v[k, :, col : col + 256]
            up = s_v[k % 2, own, col + 256 : col + 512] + sib_v[k, :, col + 256 : col + 512]
            hidden.append((gate / (1.0 + jnp.exp(-gate)) * up).astype(BF))
        hidden = jnp.concatenate(hidden, axis=1)
        hidden = jnp.dot(pack, hidden, preferred_element_type=F32).astype(BF)
        for i in range(28):
            x_v[k, i % 14, (i // 14) * 128 : (i // 14) * 128 + PACK, :] = jnp.dot(
                hidden, wd_v[:, i * 256 : (i + 1) * 256], preferred_element_type=F32
            ).astype(BF)

        def block(tq, i):
            n = tq * 7 + i
            return x_v.at[k, n % 14, pl.ds(pl.multiple_of((n // 14) * 128, 128), PACK)]

        @pl.when(c == 0)
        def _():
            for i in range(7):
                for core in range(2):
                    tq = 2 * (1 - h) + core
                    remote(
                        block(tq, i), half_v.at[k, 1, i], psend_sem.at[k], hrecv_sem.at[k], (w, tq)
                    ).start()
                pltpu.make_async_copy(block(2 * h, i), half_v.at[k, 0, i], psend_sem.at[k]).start()
                remote(
                    block(2 * h + 1, i), half_v.at[k, 0, i], psend_sem.at[k], near_sem.at[k], sibling
                ).start()

        @pl.when(c == 1)
        def _():
            for i in range(7):
                for tq in (0, 2, 1, 3):
                    remote(
                        block(tq, i), half_v.at[k, 2 + h, i], psend_sem.at[k], hrecv_sem.at[k],
                        (wide_of(1, 0, 0), tq),
                    ).start()

    def finish(k):
        part = x_v.at[k, :, pl.ds(0, 2 * PACK)]
        pltpu.make_async_copy(part, part, psend_sem.at[k]).wait()
        part = half_v.at[k, pl.ds(1, 3)]
        pltpu.make_async_copy(part, part, hrecv_sem.at[k]).wait()

        @pl.when(c == 1)
        def _():
            part = half_v.at[k, 0]
            pltpu.make_async_copy(part, part, near_sem.at[k]).wait()

        tn = (((0,), (0,)), ((), ()))
        for far in range(2):
            for i in range(7):
                both = half_v[k, 2 * far, i].astype(F32) + half_v[k, 2 * far + 1, i].astype(F32)
                x_v[k, far * 7 + i, 0:128, :] = lax.dot_general(
                    pack, both.astype(BF), tn, preferred_element_type=F32
                ).astype(BF)
        for low, many in ((0, 4), (4, 3), (7, 4), (11, 3)):
            for a in range(4):
                n = wide_of(0, 8 - a - k, 4 - a)
                src = x_v.at[k, pl.ds(low, many), pl.ds(a * 32, 32)]
                dst = back_v.at[k * 4 + a, pl.ds(low, many)]

                def away():
                    remote(src, dst, ysend_sem.at[k], yrecv_sem.at[k], (n, t)).start()

                if a > 0:
                    away()
                else:
                    @pl.when(k == 0)
                    def _():
                        pltpu.make_async_copy(src, dst, ysend_sem.at[k]).start()

                    pl.when(k > 0)(away)

    def expert_step(k, carry):
        @pl.when(k < 4)
        def _():
            gate_and_up(k)

        @pl.when(k < 2)
        def _():
            send_tokens(k + 2)

        @pl.when(k < 4)
        def _():
            down(k)

        @pl.when(k == 0)
        def _():
            part = q_v.at[pl.ds(1, 31)]
            pltpu.make_async_copy(part, part, qrecv_sem).wait()
            part = new_v.at[pl.ds(1, 31)]
            pltpu.make_async_copy(part, part, nrecv_sem).wait()

        @pl.when(k > 0)
        def _():
            finish(k - 1)

        @pl.when(k < 4)
        def _():
            lax.fori_loop(k * 8, k * 8 + 8, attend, 0)

        return carry

    lax.fori_loop(0, 5, expert_step, 0)

    acc_v[...] = jnp.zeros_like(acc_v)

    def mix(k, carry):
        part = x_v.at[k, :, pl.ds(0, 128)]
        pltpu.make_async_copy(part, part, ysend_sem.at[k]).wait()

        @pl.when(k == 0)
        def _():
            part = back_v.at[pl.ds(1, 3)]
            pltpu.make_async_copy(part, part, yrecv_sem.at[k]).wait()

        @pl.when(k > 0)
        def _():
            part = back_v.at[pl.ds(k * 4, 4)]
            pltpu.make_async_copy(part, part, yrecv_sem.at[k]).wait()

        parts = []
        for far in range(2):
            for a in range(4):
                e = wide_of(far, a + k, a)
                parts.append(jnp.where(row_id == dest_v[pl.ds(e, 1), :], mixw_v[pl.ds(e, 1), :], 0.0))
        weights = jnp.concatenate(parts, axis=0)
        high = weights.astype(BF)
        low = (weights - high.astype(F32)).astype(BF)
        tn = (((0,), (0,)), ((), ()))
        for i in range(7):
            rows = jnp.concatenate([back_v[k * 4 + a, far * 7 + i] for far in range(2) for a in range(4)], axis=0)
            acc_v[:, i * 256 : (i + 1) * 256] += lax.dot_general(
                high, rows, tn, preferred_element_type=F32
            ) + lax.dot_general(low, rows, tn, preferred_element_type=F32)
        return carry

    lax.fori_loop(0, 4, mix, 0)
    moe_out[...] = acc_v[...].astype(BF)

    part = q_v.at[pl.ds(1, 31)]
    pltpu.make_async_copy(part, part, qsend_sem).wait()
    part = new_v.at[pl.ds(1, 31)]
    pltpu.make_async_copy(part, part, nsend_sem).wait()
    part = ctx_v.at[pl.ds(1, 31)]
    pltpu.make_async_copy(part, part, csend_sem).wait()
    pltpu.make_async_copy(part, part, crecv_sem).wait()
    pltpu.make_async_copy(ctx_v.at[0], attn_out.at[w], self_sem).wait()
    part = near_v.at[pl.ds(1, 3)]
    pltpu.make_async_copy(part, part, tsend_sem).wait()
    part = tok_v.at[pl.ds(96, 288)]
    pltpu.make_async_copy(part, part, gsend_sem).wait()
    part = same_v.at[:, :, pl.ds(0, 96)]
    pltpu.make_async_copy(part, part, dsend_sem.at[0]).wait()
    pltpu.make_async_copy(other_v, other_v, dsend_sem.at[1]).wait()
    for k in range(2, 4):
        swap_sums(k).wait_send()


def shards(
    cache, queries, new_latent, cache_len, owner, moe_tokens, expert_ids, gate_weights, w_gate, w_up, w_down
):
    packed = jnp.pad(new_latent[0], ((0, 0), (0, 0), (0, 64))).reshape(32, 15, 128)
    packed = jnp.pad(packed, ((0, 0), (0, 1), (0, 0)))
    ids = expert_ids.transpose(0, 2, 1)
    gates = gate_weights.transpose(0, 2, 1)

    hbm = pl.BlockSpec(memory_space=pl.ANY)
    vmem = pl.BlockSpec(memory_space=pltpu.VMEM)
    smem = pl.BlockSpec(memory_space=pltpu.SMEM)
    dma = pltpu.SemaphoreType.DMA
    attn, moe = pl.pallas_call(
        kernel,
        out_shape=(
            jax.ShapeDtypeStruct((32, 48, 512), BF),
            jax.ShapeDtypeStruct((96, QUART), BF),
        ),
        in_specs=[hbm, hbm, hbm, hbm, vmem, vmem, smem, smem, hbm, hbm, hbm],
        out_specs=(hbm, vmem),
        scratch_shapes=[
            pltpu.VMEM((32, 576, 256), BF),
            pltpu.VMEM((32, 48, 576), BF),
            pltpu.VMEM((32, 16, 128), BF),
            pltpu.VMEM((32, 48, 512), BF),
            pltpu.VMEM((384, HALF), BF),
            pltpu.VMEM((32, 96), F32),
            pltpu.VMEM((32, 96), F32),
            pltpu.VMEM((4, 32, 96), F32),
            pltpu.VMEM((32, 384), F32),
            pltpu.VMEM((4, 14, 128, 256), BF),
            pltpu.VMEM((4, 14, 128, 256), BF),
            pltpu.VMEM((4, 14, 256, 256), BF),
            pltpu.VMEM((2, HALF, 256), BF),
            pltpu.VMEM((2, HALF, 256), BF),
            pltpu.VMEM((512, 7168), BF),
            pltpu.VMEM((2, 256, 1024), F32),
            pltpu.VMEM((4, 128, 1024), F32),
            pltpu.VMEM((4, 4, 7, PACK, 256), BF),
            pltpu.VMEM((16, 14, 32, 256), BF),
            pltpu.VMEM((96, QUART), F32),
            dma((4,)), dma((3,)), dma((3,)), dma((3,)), dma, dma, dma, dma,
            dma, dma, dma, dma, dma, dma, dma((2,)), dma((4,)), dma((2,)), dma((4,)), dma((4,)), dma((4,)), dma((4,)),
            dma((4,)), dma((4,)), dma,
        ],
        compiler_params=pltpu.CompilerParams(
            collective_id=0, has_side_effects=True, vmem_limit_bytes=64 * 1024 * 1024 - 65536
        ),
        cost_estimate=pl.CostEstimate(flops=13_000_000_000, bytes_accessed=60_000_000, transcendentals=2_000_000),
        name="handover_attend_experts",
    )(
        queries[0].reshape(32, 48, 576), packed, cache.transpose(0, 2, 1), moe_tokens.reshape(96, 7168), ids, gates, owner, cache_len,
        w_gate[0], w_up[0], w_down[0],
    )
    return attn.reshape(1, 32, 3, 16, 512), moe.reshape(3, 32, QUART)


def solution(mesh):
    in_specs = (
        P("wide", None, None),
        P("wide", None, None, "tp", None),
        P("wide", None, None, None),
        P(),
        P(),
        P(None, "wide", None),
        P(None, "wide", None),
        P(None, "wide", None),
        P("wide", None, "tp"),
        P("wide", None, "tp"),
        P("wide", "tp", None),
    )
    out_specs = (P("wide", None, None, "tp", None), P(None, "wide", "tp"))
    return jax.shard_map(shards, mesh=mesh, in_specs=in_specs, out_specs=out_specs, check_vma=False)
```

```python
import jax
import jax.numpy as jnp
from jax import lax
from jax.experimental import pallas as pl
from jax.experimental.pallas import tpu as pltpu
from jax.sharding import PartitionSpec as P

MESH = pl.DeviceIdType.MESH
BF = jnp.bfloat16
F32 = jnp.float32
SCALE = 192.0 ** (-0.5)
MASKED = -1e30
HALF = 3584
QUART = 1792
CAP = 9
ROWS = 27
PACK = 112


def offsets(j):
    a, b, far = j % 4, (j // 4) % 4, j // 16
    return (a + b + far) % 2, (a + b) % 4, a


def kernel(
    q_hbm, new_hbm, cache_hbm, tok_hbm, ids_ref, gate_ref, owner_ref, length_ref, wg_hbm, wu_hbm, wd_hbm,
    attn_out, moe_out,
    cache_v, q_v, new_v, ctx_v, tok_v, dest_v, mixw_v, near_v, picks_v, newin_v, newout_v,
    same_v, other_v, x_v, wg_v, wu_v, wd_v, s_v, sib_v, half_v, back_v, acc_v,
    load_sem, wload_sem, wsend_sem, wrecv_sem, qsend_sem, qrecv_sem, nsend_sem, nrecv_sem,
    csend_sem, crecv_sem, gsend_sem, grecv_sem, tsend_sem, trecv_sem, dsend_sem, drecv_sem, ssend_sem, srecv_sem, psend_sem, hrecv_sem, near_sem,
    ysend_sem, yrecv_sem, self_sem,
):
    w = lax.axis_index("wide")
    t = lax.axis_index("tp")
    xl, z, y = w // 16, (w // 4) % 4, w % 4
    h, c = t // 2, t % 2
    sibling = (w, h * 2 + 1 - c)

    def wide_of(far, zz, yy):
        return ((xl + far) % 2) * 16 + ((z + zz) % 4) * 4 + (y + yy) % 4

    mine = pl.ds(pl.multiple_of(c * HALF, 128), HALF)
    theirs = pl.ds(pl.multiple_of((1 - c) * HALF, 128), HALF)
    loads = [
        pltpu.make_async_copy(tok_hbm.at[:, mine], tok_v.at[pl.ds(0, 96)], load_sem.at[0]),
        pltpu.make_async_copy(cache_hbm, cache_v, load_sem.at[1]),
        pltpu.make_async_copy(q_hbm.at[w], q_v.at[0], load_sem.at[2]),
        pltpu.make_async_copy(new_hbm, newin_v, load_sem.at[3]),
    ]
    for load in loads:
        load.start()
    hidden_rows = pl.ds(pl.multiple_of(c * 256, 256), 256)
    wloads = [
        pltpu.make_async_copy(wg_hbm.at[mine], wg_v.at[c], wload_sem.at[0]),
        pltpu.make_async_copy(wu_hbm.at[mine], wu_v.at[c], wload_sem.at[1]),
        pltpu.make_async_copy(wd_hbm, wd_v.at[hidden_rows], wload_sem.at[2]),
    ]
    for load in wloads:
        load.start()

    barrier = pltpu.get_barrier_semaphore()

    def greet(n, tq):
        pl.semaphore_signal(barrier, inc=1, device_id=(n, tq), device_id_type=MESH)

    def greet_wide(i, carry):
        greet((w + i) % 32, t)
        return carry

    lax.fori_loop(1, 32, greet_wide, 0)
    for i in range(4):
        greet(wide_of(1, i, 0), (1 - h) * 2 + c)
    for i in range(1, 4):
        greet(wide_of(1, 0, i), (1 - h) * 2 + c)
        greet(w, (t + i) % 4)
    for i in range(2):
        greet(wide_of(1, 0, 0), i * 2 + 1 - c)

    expert = lax.broadcasted_iota(jnp.int32, (32, 96), 0)
    token = lax.broadcasted_iota(jnp.int32, (32, 96), 1)
    hits = jnp.zeros((32, 96), F32)
    mixw = jnp.zeros((32, 96), F32)
    ids = jnp.concatenate([ids_ref[i] for i in range(3)], axis=1)
    gates = jnp.concatenate([gate_ref[i] for i in range(3)], axis=1)
    for k in range(8):
        equal = expert == ids[k : k + 1, :]
        hits = jnp.where(equal, 1.0, hits)
        mixw = jnp.where(equal, gates[k : k + 1, :], mixw)
    first = lax.broadcasted_iota(jnp.int32, (96, 96), 0)
    later = lax.broadcasted_iota(jnp.int32, (96, 96), 1)
    before = ((first // 32 == later // 32) & (first < later)).astype(F32)
    rank = jnp.dot(hits, before, preferred_element_type=F32)
    place = (token // 32).astype(F32) * CAP + rank
    dest_v[...] = jnp.where(hits > 0.0, place, -1.0)
    near_v[0] = dest_v[...]
    mixw_v[...] = mixw
    row_id = lax.broadcasted_iota(jnp.int32, (32, 96), 0).astype(F32)

    packed_id = lax.broadcasted_iota(jnp.int32, (PACK, 128), 0)
    padded_id = lax.broadcasted_iota(jnp.int32, (PACK, 128), 1)
    pack = (packed_id == (padded_id // 32) * ROWS + padded_id % 32) & (padded_id % 32 < ROWS)
    pack = jnp.where(pack, 1.0, 0.0).astype(BF)

    loads[3].wait()
    pieces = []
    for i in range(3):
        for j in range(5):
            piece = newin_v[i, :, j * 128 : min(j * 128 + 128, 576)]
            if j == 4:
                piece = jnp.concatenate([piece, jnp.zeros((32, 64), BF)], axis=1)
            pieces.append(piece)
    to_row = lax.broadcasted_iota(jnp.int32, (512, 480), 0)
    from_row = lax.broadcasted_iota(jnp.int32, (512, 480), 1)
    moved = (to_row // 16 == from_row % 32) & (to_row % 16 == from_row // 32)
    rows = jnp.dot(
        jnp.where(moved, 1.0, 0.0).astype(BF), jnp.concatenate(pieces, axis=0), preferred_element_type=F32
    ).astype(BF)
    for i in range(32):
        newout_v[i] = rows[i * 16 : i * 16 + 16]
    new_v[0] = newout_v[w]

    pl.semaphore_wait(barrier, 43)

    def remote(src, dst, send, recv, dev):
        return pltpu.make_async_remote_copy(
            src_ref=src, dst_ref=dst, send_sem=send, recv_sem=recv, device_id=dev, device_id_type=MESH
        )

    for d in range(1, 4):
        peer = (wide_of(0, (1 - c) * d, c * d), t)
        remote(near_v.at[0], near_v.at[d], tsend_sem, trecv_sem, peer).start()
    for part in range(4):
        for d in range(1, 4):
            peer = (wide_of(0, (1 - c) * d, c * d), t)
            cols = pl.ds(part * 896, 896)
            remote(
                tok_hbm.at[:, pl.ds(pl.multiple_of(c * HALF + part * 896, 128), 896)],
                tok_v.at[pl.ds(d * 96, 96), cols], gsend_sem, grecv_sem, peer,
            ).start()

    def send_tokens(k):
        def pick(far):
            parts = []
            for a in range(4):
                e = wide_of(far, c * (a + k), (1 - c) * a)
                held = (a + (1 - c) * k) % 4
                rows = lax.broadcasted_iota(jnp.int32, (32, 384), 0).astype(F32)
                group = lax.broadcasted_iota(jnp.int32, (32, 384), 1) // 96
                chosen = (rows == picks_v[pl.ds(e, 1), :]) & (group == held)
                parts.append(jnp.where(chosen, 1.0, 0.0))
            return jnp.concatenate(parts, axis=0).astype(BF)

        for far, out in ((0, same_v), (1, other_v)):
            picked = pick(far)
            for part in range(2):
                rows = jnp.dot(
                    picked, tok_v[:, part * QUART : (part + 1) * QUART], preferred_element_type=F32
                ).astype(BF)
                for i in range(7):
                    out[k, part * 7 + i] = rows[:, i * 256 : (i + 1) * 256]

        home = c * ((4 - k) % 4)
        kept = pl.ds(pl.multiple_of(home * 32, 32), 32)
        for i in range(14):
            x_v[k, i, kept, :] = same_v[k, i, kept, :]
        for piece in range(5):
            low, many = piece * 3, 3 if piece < 4 else 2
            far_low, far_many = ((0, 3), (3, 2), (5, 3), (8, 3), (11, 3))[piece]
            far_chip = t if piece < 2 else (1 - h) * 2 + c
            for a in range(4):
                src = pl.ds(a * 32, 32)
                away = pl.ds(128 + a * 32, 32)

                @pl.when(home != a)
                def _():
                    blocks = pl.ds(low, many)
                    remote(
                        same_v.at[k, blocks, src], x_v.at[k, blocks, src], dsend_sem.at[k], drecv_sem.at[k],
                        (wide_of(0, c * (a + k), (1 - c) * a), t),
                    ).start()

                blocks = pl.ds(far_low, far_many)
                remote(
                    other_v.at[k, blocks, src], x_v.at[k, blocks, away], dsend_sem.at[4], drecv_sem.at[k],
                    (wide_of(1, c * (a + k), (1 - c) * a), far_chip),
                ).start()

    swaps = [
        remote(wg_hbm.at[theirs], wg_v.at[c], wsend_sem.at[0], wrecv_sem.at[0], sibling),
        remote(wu_hbm.at[theirs], wu_v.at[c], wsend_sem.at[1], wrecv_sem.at[1], sibling),
        remote(wd_hbm, wd_v.at[hidden_rows], wsend_sem.at[2], wrecv_sem.at[2], sibling),
    ]
    for swap in swaps:
        swap.start()

    def send_query(j, carry):
        far, zz, yy = offsets(j)
        n = wide_of(far, zz, yy)
        remote(q_hbm.at[n], q_v.at[j], qsend_sem, qrecv_sem, (n, t)).start()
        remote(newout_v.at[n], new_v.at[j], nsend_sem, nrecv_sem, (n, t)).start()
        return carry

    lax.fori_loop(1, 16, send_query, 0)
    loads[0].wait()
    part = near_v.at[pl.ds(1, 3)]
    pltpu.make_async_copy(part, part, trecv_sem).wait()
    part = tok_v.at[pl.ds(96, 288)]
    pltpu.make_async_copy(part, part, grecv_sem).wait()
    picks_v[...] = jnp.concatenate([near_v[i] for i in range(4)], axis=1)
    send_tokens(0)
    send_tokens(1)
    lax.fori_loop(16, 32, send_query, 0)

    for load in loads[1:3]:
        load.wait()
    for load in wloads:
        load.wait()
    for swap in swaps:
        swap.wait()

    def attend(j, carry):
        far, zz, yy = offsets(j)
        o = wide_of(far, 4 - zz, 4 - yy)

        def find(r, found):
            return jnp.where(owner_ref[w * 32 + r] == o, r, found)

        held = lax.fori_loop(0, 32, find, 0)
        length = length_ref[w * 32 + held]
        latents = cache_v[held]
        query = q_v[j]
        packed = new_v[j]
        r16 = lax.broadcasted_iota(jnp.int32, (16, 16), 0)
        c16 = lax.broadcasted_iota(jnp.int32, (16, 16), 1)
        pieces = [
            jnp.dot(
                jnp.where((c16 == r16 * 5 + i) & (r16 < 3), 1.0, 0.0).astype(BF), packed,
                preferred_element_type=F32,
            ).astype(BF)
            for i in range(5)
        ]
        fresh_key = jnp.concatenate(pieces[:4], axis=1)
        nt = (((1,), (1,)), ((), ()))
        scores = jnp.dot(query, latents, preferred_element_type=F32) * SCALE
        fresh = lax.dot_general(query[:, :512], fresh_key, nt, preferred_element_type=F32)
        fresh += lax.dot_general(query[:, 512:], pieces[4][:, :64], nt, preferred_element_type=F32)
        fresh = fresh * SCALE
        valid = lax.broadcasted_iota(jnp.int32, (48, 256), 1) < length
        step = lax.broadcasted_iota(jnp.int32, (48, 16), 0) // 16
        fresh_valid = lax.broadcasted_iota(jnp.int32, (48, 16), 1) <= step
        scores = jnp.where(valid, scores, MASKED)
        fresh = jnp.where(fresh_valid, fresh, MASKED)
        top = jnp.maximum(
            jnp.max(scores, axis=1, keepdims=True), jnp.max(fresh, axis=1, keepdims=True)
        )
        weights = jnp.where(valid, jnp.exp(scores - top), 0.0)
        fresh_weights = jnp.where(fresh_valid, jnp.exp(fresh - top), 0.0)
        total = jnp.sum(weights, axis=1, keepdims=True) + jnp.sum(fresh_weights, axis=1, keepdims=True)
        context = lax.dot_general(weights.astype(BF), latents[:512, :], nt, preferred_element_type=F32)
        context += jnp.dot(fresh_weights.astype(BF), fresh_key, preferred_element_type=F32)
        ctx_v[j] = (context / total).astype(BF)

        @pl.when(j == 0)
        def _():
            pltpu.make_async_copy(ctx_v.at[j], attn_out.at[w], self_sem).start()

        @pl.when(j > 0)
        def _():
            remote(ctx_v.at[j], attn_out.at[w], csend_sem, crecv_sem, (o, t)).start()

        return carry

    def swap_sums(k):
        theirs = pl.ds(pl.multiple_of((1 - c) * 128, 128), 128)
        return remote(s_v.at[k % 2, theirs], sib_v.at[k], ssend_sem.at[k % 2], srecv_sem.at[k], sibling)

    def gate_and_up(k):
        part = x_v.at[k, :, pl.ds(0, 224)]
        pltpu.make_async_copy(part, part, drecv_sem.at[k]).wait()

        @pl.when(k >= 2)
        def _():
            swap_sums(k).wait_send()

        rows = jnp.concatenate([x_v[k, i] for i in range(14)], axis=1)
        for core in range(2):
            for i, weight in enumerate((wg_v, wu_v)):
                col = core * 512 + i * 256
                s_v[k % 2, :, col : col + 256] = jnp.dot(rows, weight[core], preferred_element_type=F32)
        swap_sums(k).start()

    def down(k):
        swap_sums(k).wait_recv()
        own = pl.ds(pl.multiple_of(c * 128, 128), 128)
        hidden = []
        for core in range(2):
            col = core * 512
            gate = s_v[k % 2, own, col : col + 256] + sib_v[k, :, col : col + 256]
            up = s_v[k % 2, own, col + 256 : col + 512] + sib_v[k, :, col + 256 : col + 512]
            hidden.append((gate / (1.0 + jnp.exp(-gate)) * up).astype(BF))
        hidden = jnp.concatenate(hidden, axis=1)
        hidden = jnp.dot(pack, hidden, preferred_element_type=F32).astype(BF)
        for i in range(28):
            x_v[k, i % 14, (i // 14) * 128 : (i // 14) * 128 + PACK, :] = jnp.dot(
                hidden, wd_v[:, i * 256 : (i + 1) * 256], preferred_element_type=F32
            ).astype(BF)

        def block(tq, i):
            n = tq * 7 + i
            return x_v.at[k, n % 14, pl.ds(pl.multiple_of((n // 14) * 128, 128), PACK)]

        @pl.when(c == 0)
        def _():
            for i in range(7):
                p = i // 4
                for core in range(2):
                    tq = 2 * (1 - h) + core
                    remote(
                        block(tq, i), half_v.at[k, 1, i], psend_sem.at[k], hrecv_sem.at[p, k], (w, tq)
                    ).start()
                pltpu.make_async_copy(block(2 * h, i), half_v.at[k, 0, i], near_sem.at[p, k]).start()
                remote(
                    block(2 * h + 1, i), half_v.at[k, 0, i], psend_sem.at[k], near_sem.at[p, k], sibling
                ).start()

        @pl.when(c == 1)
        def _():
            for i in range(7):
                for tq in (0, 2, 1, 3):
                    remote(
                        block(tq, i), half_v.at[k, 2 + h, i], psend_sem.at[k], hrecv_sem.at[i // 4, k],
                        (wide_of(1, 0, 0), tq),
                    ).start()

    def finish(k, low, many, part_id):
        part = half_v.at[k, pl.ds(1, 3), pl.ds(low, many)]
        pltpu.make_async_copy(part, part, hrecv_sem.at[part_id, k]).wait()
        part = half_v.at[k, 0, pl.ds(low, many)]
        pltpu.make_async_copy(part, part, near_sem.at[part_id, k]).wait()
        tn = (((0,), (0,)), ((), ()))
        for far in range(2):
            for i in range(low, low + many):
                both = half_v[k, 2 * far, i].astype(F32) + half_v[k, 2 * far + 1, i].astype(F32)
                same_v[k, far * 7 + i] = lax.dot_general(
                    pack, both.astype(BF), tn, preferred_element_type=F32
                ).astype(BF)
        for far in range(2):
            for a in range(4):
                n = wide_of(0, 8 - a - k, 4 - a)
                blocks = pl.ds(far * 7 + low, many)
                src = same_v.at[k, blocks, pl.ds(a * 32, 32)]
                dst = back_v.at[k * 4 + a, blocks]

                def away():
                    remote(src, dst, ysend_sem.at[k], yrecv_sem.at[k], (n, t)).start()

                if a > 0:
                    away()
                else:
                    @pl.when(k == 0)
                    def _():
                        pltpu.make_async_copy(src, dst, ysend_sem.at[k]).start()

                    pl.when(k > 0)(away)

    def expert_step(k, carry):
        @pl.when(k < 4)
        def _():
            gate_and_up(k)

        @pl.when(k < 2)
        def _():
            send_tokens(k + 2)

        @pl.when(k < 4)
        def _():
            down(k)

        @pl.when(k == 0)
        def _():
            part = q_v.at[pl.ds(1, 31)]
            pltpu.make_async_copy(part, part, qrecv_sem).wait()
            part = new_v.at[pl.ds(1, 31)]
            pltpu.make_async_copy(part, part, nrecv_sem).wait()

        @pl.when(k > 0)
        def _():
            part = same_v.at[k - 1, :, pl.ds(0, 96)]
            pltpu.make_async_copy(part, part, dsend_sem.at[k - 1]).wait()
            finish(k - 1, 0, 4, 0)
            finish(k - 1, 4, 3, 1)

        @pl.when(k < 4)
        def _():
            lax.fori_loop(k * 8, k * 8 + 8, attend, 0)

        return carry

    lax.fori_loop(0, 5, expert_step, 0)

    acc_v[...] = jnp.zeros_like(acc_v)

    def mix(k, carry):
        part = same_v.at[k]
        pltpu.make_async_copy(part, part, ysend_sem.at[k]).wait()

        @pl.when(k == 0)
        def _():
            part = back_v.at[pl.ds(1, 3)]
            pltpu.make_async_copy(part, part, yrecv_sem.at[k]).wait()

        @pl.when(k > 0)
        def _():
            part = back_v.at[pl.ds(k * 4, 4)]
            pltpu.make_async_copy(part, part, yrecv_sem.at[k]).wait()

        parts = []
        for far in range(2):
            for a in range(4):
                e = wide_of(far, a + k, a)
                parts.append(jnp.where(row_id == dest_v[pl.ds(e, 1), :], mixw_v[pl.ds(e, 1), :], 0.0))
        weights = jnp.concatenate(parts, axis=0)
        high = weights.astype(BF)
        low = (weights - high.astype(F32)).astype(BF)
        tn = (((0,), (0,)), ((), ()))
        for i in range(7):
            rows = jnp.concatenate([back_v[k * 4 + a, far * 7 + i] for far in range(2) for a in range(4)], axis=0)
            acc_v[:, i * 256 : (i + 1) * 256] += lax.dot_general(
                high, rows, tn, preferred_element_type=F32
            ) + lax.dot_general(low, rows, tn, preferred_element_type=F32)
        return carry

    lax.fori_loop(0, 4, mix, 0)
    moe_out[...] = acc_v[...].astype(BF)

    part = q_v.at[pl.ds(1, 31)]
    pltpu.make_async_copy(part, part, qsend_sem).wait()
    part = new_v.at[pl.ds(1, 31)]
    pltpu.make_async_copy(part, part, nsend_sem).wait()
    part = ctx_v.at[pl.ds(1, 31)]
    pltpu.make_async_copy(part, part, csend_sem).wait()
    pltpu.make_async_copy(part, part, crecv_sem).wait()
    pltpu.make_async_copy(ctx_v.at[0], attn_out.at[w], self_sem).wait()
    part = near_v.at[pl.ds(1, 3)]
    pltpu.make_async_copy(part, part, tsend_sem).wait()
    part = tok_v.at[pl.ds(96, 288)]
    pltpu.make_async_copy(part, part, gsend_sem).wait()
    pltpu.make_async_copy(other_v, other_v, dsend_sem.at[4]).wait()
    for k in range(2, 4):
        swap_sums(k).wait_send()
    for k in range(4):
        @pl.when(c == 0)
        def _():
            part = half_v.at[k, pl.ds(0, 3)]
            pltpu.make_async_copy(part, part, psend_sem.at[k]).wait()

        @pl.when(c == 1)
        def _():
            part = half_v.at[k]
            pltpu.make_async_copy(part, part, psend_sem.at[k]).wait()


def shards(
    cache, queries, new_latent, cache_len, owner, moe_tokens, expert_ids, gate_weights, w_gate, w_up, w_down
):
    ids = expert_ids.transpose(0, 2, 1)
    gates = gate_weights.transpose(0, 2, 1)

    hbm = pl.BlockSpec(memory_space=pl.ANY)
    vmem = pl.BlockSpec(memory_space=pltpu.VMEM)
    smem = pl.BlockSpec(memory_space=pltpu.SMEM)
    dma = pltpu.SemaphoreType.DMA
    attn, moe = pl.pallas_call(
        kernel,
        out_shape=(
            jax.ShapeDtypeStruct((32, 48, 512), BF),
            jax.ShapeDtypeStruct((96, QUART), BF),
        ),
        in_specs=[hbm, hbm, hbm, hbm, vmem, vmem, smem, smem, hbm, hbm, hbm],
        out_specs=(hbm, vmem),
        scratch_shapes=[
            pltpu.VMEM((32, 576, 256), BF),
            pltpu.VMEM((32, 48, 576), BF),
            pltpu.VMEM((32, 16, 128), BF),
            pltpu.VMEM((32, 48, 512), BF),
            pltpu.VMEM((384, HALF), BF),
            pltpu.VMEM((32, 96), F32),
            pltpu.VMEM((32, 96), F32),
            pltpu.VMEM((4, 32, 96), F32),
            pltpu.VMEM((32, 384), F32),
            pltpu.VMEM((3, 32, 576), BF),
            pltpu.VMEM((32, 16, 128), BF),
            pltpu.VMEM((4, 14, 128, 256), BF),
            pltpu.VMEM((4, 14, 128, 256), BF),
            pltpu.VMEM((4, 14, 256, 256), BF),
            pltpu.VMEM((2, HALF, 256), BF),
            pltpu.VMEM((2, HALF, 256), BF),
            pltpu.VMEM((512, 7168), BF),
            pltpu.VMEM((2, 256, 1024), F32),
            pltpu.VMEM((4, 128, 1024), F32),
            pltpu.VMEM((4, 4, 7, PACK, 256), BF),
            pltpu.VMEM((16, 14, 32, 256), BF),
            pltpu.VMEM((96, QUART), F32),
            dma((4,)), dma((3,)), dma((3,)), dma((3,)), dma, dma, dma, dma,
            dma, dma, dma, dma, dma, dma, dma((5,)), dma((4,)), dma((2,)), dma((4,)), dma((4,)), dma((2, 4)), dma((2, 4)),
            dma((4,)), dma((4,)), dma,
        ],
        compiler_params=pltpu.CompilerParams(
            collective_id=0, has_side_effects=True, vmem_limit_bytes=64 * 1024 * 1024 - 65536
        ),
        cost_estimate=pl.CostEstimate(flops=13_000_000_000, bytes_accessed=60_000_000, transcendentals=2_000_000),
        name="handover_attend_experts",
    )(
        queries[0].reshape(32, 48, 576), new_latent[0].transpose(1, 0, 2), cache.transpose(0, 2, 1), moe_tokens.reshape(96, 7168), ids, gates, owner, cache_len,
        w_gate[0], w_up[0], w_down[0],
    )
    return attn.reshape(1, 32, 3, 16, 512), moe.reshape(3, 32, QUART)


def solution(mesh):
    in_specs = (
        P("wide", None, None),
        P("wide", None, None, "tp", None),
        P("wide", None, None, None),
        P(),
        P(),
        P(None, "wide", None),
        P(None, "wide", None),
        P(None, "wide", None),
        P("wide", None, "tp"),
        P("wide", None, "tp"),
        P("wide", "tp", None),
    )
    out_specs = (P("wide", None, None, "tp", None), P(None, "wide", "tp"))
    return jax.shard_map(shards, mesh=mesh, in_specs=in_specs, out_specs=out_specs, check_vma=False)
```

```python
import jax
import jax.numpy as jnp
from jax import lax
from jax.experimental import pallas as pl
from jax.experimental.pallas import tpu as pltpu
from jax.sharding import PartitionSpec as P

MESH = pl.DeviceIdType.MESH
BF = jnp.bfloat16
F32 = jnp.float32
SCALE = 192.0 ** (-0.5)
MASKED = -1e30
HALF = 3584
QUART = 1792
CAP = 9
ROWS = 27
PACK = 112
PART_OF = (0, 0, 1, 1, 2, 2, 3)


def offsets(j):
    a, b, far = j % 4, (j // 4) % 4, j // 16
    return (a + b + far) % 2, (a + b) % 4, a


def kernel(
    q_hbm, new_hbm, cache_hbm, tok_hbm, ids_ref, gate_ref, owner_ref, length_ref, wg_hbm, wu_hbm, wd_hbm,
    attn_out, moe_out,
    cache_v, q_v, new_v, ctx_v, tok_v, dest_v, mixw_v, near_v, picks_v, newin_v, newout_v,
    same_v, other_v, x_v, wg_v, wu_v, wd_v, s_v, sib_v, half_v, back_v, acc_v,
    load_sem, wload_sem, wsend_sem, wrecv_sem, qsend_sem, qrecv_sem, nsend_sem, nrecv_sem,
    csend_sem, crecv_sem, gsend_sem, grecv_sem, tsend_sem, trecv_sem, dsend_sem, drecv_sem, ssend_sem, srecv_sem, psend_sem, hrecv_sem, near_sem,
    ysend_sem, yrecv_sem, self_sem,
):
    w = lax.axis_index("wide")
    t = lax.axis_index("tp")
    xl, z, y = w // 16, (w // 4) % 4, w % 4
    h, c = t // 2, t % 2
    sibling = (w, h * 2 + 1 - c)

    def wide_of(far, zz, yy):
        return ((xl + far) % 2) * 16 + ((z + zz) % 4) * 4 + (y + yy) % 4

    mine = pl.ds(pl.multiple_of(c * HALF, 128), HALF)
    theirs = pl.ds(pl.multiple_of((1 - c) * HALF, 128), HALF)
    loads = [
        pltpu.make_async_copy(tok_hbm.at[:, mine], tok_v.at[pl.ds(0, 96)], load_sem.at[0]),
        pltpu.make_async_copy(cache_hbm, cache_v, load_sem.at[1]),
        pltpu.make_async_copy(q_hbm.at[w], q_v.at[0], load_sem.at[2]),
        pltpu.make_async_copy(new_hbm, newin_v, load_sem.at[3]),
    ]
    for load in loads:
        load.start()
    hidden_rows = pl.ds(pl.multiple_of(c * 256, 256), 256)
    wloads = [
        pltpu.make_async_copy(wg_hbm.at[mine], wg_v.at[c], wload_sem.at[0]),
        pltpu.make_async_copy(wu_hbm.at[mine], wu_v.at[c], wload_sem.at[1]),
        pltpu.make_async_copy(wd_hbm, wd_v.at[hidden_rows], wload_sem.at[2]),
    ]
    for load in wloads:
        load.start()

    barrier = pltpu.get_barrier_semaphore()

    def greet(n, tq):
        pl.semaphore_signal(barrier, inc=1, device_id=(n, tq), device_id_type=MESH)

    def greet_wide(i, carry):
        greet((w + i) % 32, t)
        return carry

    lax.fori_loop(1, 32, greet_wide, 0)
    for i in range(4):
        greet(wide_of(1, i, 0), (1 - h) * 2 + c)
    for i in range(1, 4):
        greet(wide_of(1, 0, i), (1 - h) * 2 + c)
        greet(w, (t + i) % 4)
    for i in range(2):
        greet(wide_of(1, 0, 0), i * 2 + 1 - c)

    expert = lax.broadcasted_iota(jnp.int32, (32, 96), 0)
    token = lax.broadcasted_iota(jnp.int32, (32, 96), 1)
    hits = jnp.zeros((32, 96), F32)
    mixw = jnp.zeros((32, 96), F32)
    ids = jnp.concatenate([ids_ref[i] for i in range(3)], axis=1)
    gates = jnp.concatenate([gate_ref[i] for i in range(3)], axis=1)
    for k in range(8):
        equal = expert == ids[k : k + 1, :]
        hits = jnp.where(equal, 1.0, hits)
        mixw = jnp.where(equal, gates[k : k + 1, :], mixw)
    first = lax.broadcasted_iota(jnp.int32, (96, 96), 0)
    later = lax.broadcasted_iota(jnp.int32, (96, 96), 1)
    before = ((first // 32 == later // 32) & (first < later)).astype(F32)
    rank = jnp.dot(hits, before, preferred_element_type=F32)
    place = (token // 32).astype(F32) * CAP + rank
    dest_v[...] = jnp.where(hits > 0.0, place, -1.0)
    near_v[0] = dest_v[...]
    mixw_v[...] = mixw
    row_id = lax.broadcasted_iota(jnp.int32, (32, 96), 0).astype(F32)

    packed_id = lax.broadcasted_iota(jnp.int32, (PACK, 128), 0)
    padded_id = lax.broadcasted_iota(jnp.int32, (PACK, 128), 1)
    pack = (packed_id == (padded_id // 32) * ROWS + padded_id % 32) & (padded_id % 32 < ROWS)
    pack = jnp.where(pack, 1.0, 0.0).astype(BF)

    loads[3].wait()
    pieces = []
    for i in range(3):
        for j in range(5):
            piece = newin_v[i, :, j * 128 : min(j * 128 + 128, 576)]
            if j == 4:
                piece = jnp.concatenate([piece, jnp.zeros((32, 64), BF)], axis=1)
            pieces.append(piece)
    to_row = lax.broadcasted_iota(jnp.int32, (512, 480), 0)
    from_row = lax.broadcasted_iota(jnp.int32, (512, 480), 1)
    moved = (to_row // 16 == from_row % 32) & (to_row % 16 == from_row // 32)
    rows = jnp.dot(
        jnp.where(moved, 1.0, 0.0).astype(BF), jnp.concatenate(pieces, axis=0), preferred_element_type=F32
    ).astype(BF)
    for i in range(32):
        newout_v[i] = rows[i * 16 : i * 16 + 16]
    new_v[0] = newout_v[w]

    pl.semaphore_wait(barrier, 43)

    def remote(src, dst, send, recv, dev):
        return pltpu.make_async_remote_copy(
            src_ref=src, dst_ref=dst, send_sem=send, recv_sem=recv, device_id=dev, device_id_type=MESH
        )

    for d in range(1, 4):
        peer = (wide_of(0, (1 - c) * d, c * d), t)
        remote(near_v.at[0], near_v.at[d], tsend_sem, trecv_sem, peer).start()
    for part in range(4):
        for d in range(1, 4):
            peer = (wide_of(0, (1 - c) * d, c * d), t)
            cols = pl.ds(part * 896, 896)
            remote(
                tok_hbm.at[:, pl.ds(pl.multiple_of(c * HALF + part * 896, 128), 896)],
                tok_v.at[pl.ds(d * 96, 96), cols], gsend_sem, grecv_sem, peer,
            ).start()

    def send_tokens(k):
        def pick(far):
            parts = []
            for a in range(4):
                e = wide_of(far, c * (a + k), (1 - c) * a)
                held = (a + (1 - c) * k) % 4
                rows = lax.broadcasted_iota(jnp.int32, (32, 384), 0).astype(F32)
                group = lax.broadcasted_iota(jnp.int32, (32, 384), 1) // 96
                chosen = (rows == picks_v[pl.ds(e, 1), :]) & (group == held)
                parts.append(jnp.where(chosen, 1.0, 0.0))
            return jnp.concatenate(parts, axis=0).astype(BF)

        for far, out in ((0, same_v), (1, other_v)):
            picked = pick(far)
            for part in range(2):
                rows = jnp.dot(
                    picked, tok_v[:, part * QUART : (part + 1) * QUART], preferred_element_type=F32
                ).astype(BF)
                for i in range(7):
                    out[k, part * 7 + i] = rows[:, i * 256 : (i + 1) * 256]

        home = c * ((4 - k) % 4)
        kept = pl.ds(pl.multiple_of(home * 32, 32), 32)
        for i in range(14):
            x_v[k, i, kept, :] = same_v[k, i, kept, :]
        for piece in range(4):
            low, many = ((0, 4), (4, 4), (8, 3), (11, 3))[piece]
            far_low, far_many = ((0, 5), (5, 3), (8, 3), (11, 3))[piece]
            far_chip = t if piece < 1 else (1 - h) * 2 + c
            for a in range(4):
                src = pl.ds(a * 32, 32)
                away = pl.ds(128 + a * 32, 32)

                @pl.when(home != a)
                def _():
                    blocks = pl.ds(low, many)
                    remote(
                        same_v.at[k, blocks, src], x_v.at[k, blocks, src], dsend_sem.at[k], drecv_sem.at[k],
                        (wide_of(0, c * (a + k), (1 - c) * a), t),
                    ).start()

                blocks = pl.ds(far_low, far_many)
                remote(
                    other_v.at[k, blocks, src], x_v.at[k, blocks, away], dsend_sem.at[4], drecv_sem.at[k],
                    (wide_of(1, c * (a + k), (1 - c) * a), far_chip),
                ).start()

    swaps = [
        remote(wg_hbm.at[theirs], wg_v.at[c], wsend_sem.at[0], wrecv_sem.at[0], sibling),
        remote(wu_hbm.at[theirs], wu_v.at[c], wsend_sem.at[1], wrecv_sem.at[1], sibling),
        remote(wd_hbm, wd_v.at[hidden_rows], wsend_sem.at[2], wrecv_sem.at[2], sibling),
    ]
    for swap in swaps:
        swap.start()

    def send_query(j, carry):
        far, zz, yy = offsets(j)
        n = wide_of(far, zz, yy)
        remote(q_hbm.at[n], q_v.at[j], qsend_sem, qrecv_sem, (n, t)).start()
        remote(newout_v.at[n], new_v.at[j], nsend_sem, nrecv_sem, (n, t)).start()
        return carry

    lax.fori_loop(1, 16, send_query, 0)
    loads[0].wait()
    part = near_v.at[pl.ds(1, 3)]
    pltpu.make_async_copy(part, part, trecv_sem).wait()
    part = tok_v.at[pl.ds(96, 288)]
    pltpu.make_async_copy(part, part, grecv_sem).wait()
    picks_v[...] = jnp.concatenate([near_v[i] for i in range(4)], axis=1)
    send_tokens(0)
    send_tokens(1)
    lax.fori_loop(16, 32, send_query, 0)

    for load in loads[1:3]:
        load.wait()
    for load in wloads:
        load.wait()
    for swap in swaps:
        swap.wait()

    def attend(j, carry):
        far, zz, yy = offsets(j)
        o = wide_of(far, 4 - zz, 4 - yy)

        def find(r, found):
            return jnp.where(owner_ref[w * 32 + r] == o, r, found)

        held = lax.fori_loop(0, 32, find, 0)
        length = length_ref[w * 32 + held]
        latents = cache_v[held]
        query = q_v[j]
        packed = new_v[j]
        r16 = lax.broadcasted_iota(jnp.int32, (16, 16), 0)
        c16 = lax.broadcasted_iota(jnp.int32, (16, 16), 1)
        pieces = [
            jnp.dot(
                jnp.where((c16 == r16 * 5 + i) & (r16 < 3), 1.0, 0.0).astype(BF), packed,
                preferred_element_type=F32,
            ).astype(BF)
            for i in range(5)
        ]
        fresh_key = jnp.concatenate(pieces[:4], axis=1)
        nt = (((1,), (1,)), ((), ()))
        scores = jnp.dot(query, latents, preferred_element_type=F32) * SCALE
        fresh = lax.dot_general(query[:, :512], fresh_key, nt, preferred_element_type=F32)
        fresh += lax.dot_general(query[:, 512:], pieces[4][:, :64], nt, preferred_element_type=F32)
        fresh = fresh * SCALE
        valid = lax.broadcasted_iota(jnp.int32, (48, 256), 1) < length
        step = lax.broadcasted_iota(jnp.int32, (48, 16), 0) // 16
        fresh_valid = lax.broadcasted_iota(jnp.int32, (48, 16), 1) <= step
        scores = jnp.where(valid, scores, MASKED)
        fresh = jnp.where(fresh_valid, fresh, MASKED)
        top = jnp.maximum(
            jnp.max(scores, axis=1, keepdims=True), jnp.max(fresh, axis=1, keepdims=True)
        )
        weights = jnp.where(valid, jnp.exp(scores - top), 0.0)
        fresh_weights = jnp.where(fresh_valid, jnp.exp(fresh - top), 0.0)
        total = jnp.sum(weights, axis=1, keepdims=True) + jnp.sum(fresh_weights, axis=1, keepdims=True)
        context = lax.dot_general(weights.astype(BF), latents[:512, :], nt, preferred_element_type=F32)
        context += jnp.dot(fresh_weights.astype(BF), fresh_key, preferred_element_type=F32)
        ctx_v[j] = (context / total).astype(BF)

        @pl.when(j == 0)
        def _():
            pltpu.make_async_copy(ctx_v.at[j], attn_out.at[w], self_sem).start()

        @pl.when(j > 0)
        def _():
            remote(ctx_v.at[j], attn_out.at[w], csend_sem, crecv_sem, (o, t)).start()

        return carry

    def swap_sums(k):
        theirs = pl.ds(pl.multiple_of((1 - c) * 128, 128), 128)
        return remote(s_v.at[k % 2, theirs], sib_v.at[k], ssend_sem.at[k % 2], srecv_sem.at[k], sibling)

    def gate_and_up(k):
        part = x_v.at[k, :, pl.ds(0, 224)]
        pltpu.make_async_copy(part, part, drecv_sem.at[k]).wait()

        @pl.when(k >= 2)
        def _():
            swap_sums(k).wait_send()

        rows = jnp.concatenate([x_v[k, i] for i in range(14)], axis=1)
        for core in range(2):
            for i, weight in enumerate((wg_v, wu_v)):
                col = core * 512 + i * 256
                s_v[k % 2, :, col : col + 256] = jnp.dot(rows, weight[core], preferred_element_type=F32)
        swap_sums(k).start()

    def down(k):
        swap_sums(k).wait_recv()
        own = pl.ds(pl.multiple_of(c * 128, 128), 128)
        hidden = []
        for core in range(2):
            col = core * 512
            gate = s_v[k % 2, own, col : col + 256] + sib_v[k, :, col : col + 256]
            up = s_v[k % 2, own, col + 256 : col + 512] + sib_v[k, :, col + 256 : col + 512]
            hidden.append((gate / (1.0 + jnp.exp(-gate)) * up).astype(BF))
        hidden = jnp.concatenate(hidden, axis=1)
        hidden = jnp.dot(pack, hidden, preferred_element_type=F32).astype(BF)
        for i in range(28):
            x_v[k, i % 14, (i // 14) * 128 : (i // 14) * 128 + PACK, :] = jnp.dot(
                hidden, wd_v[:, i * 256 : (i + 1) * 256], preferred_element_type=F32
            ).astype(BF)

        def block(tq, i):
            n = tq * 7 + i
            return x_v.at[k, n % 14, pl.ds(pl.multiple_of((n // 14) * 128, 128), PACK)]

        @pl.when(c == 0)
        def _():
            for i in range(7):
                p = PART_OF[i]
                for core in range(2):
                    tq = 2 * (1 - h) + core
                    remote(
                        block(tq, i), half_v.at[k, 1, i], psend_sem.at[k], hrecv_sem.at[p, k], (w, tq)
                    ).start()
                pltpu.make_async_copy(block(2 * h, i), half_v.at[k, 0, i], near_sem.at[p, k]).start()
                remote(
                    block(2 * h + 1, i), half_v.at[k, 0, i], psend_sem.at[k], near_sem.at[p, k], sibling
                ).start()

        @pl.when(c == 1)
        def _():
            for i in range(7):
                for tq in (0, 2, 1, 3):
                    remote(
                        block(tq, i), half_v.at[k, 2 + h, i], psend_sem.at[k], hrecv_sem.at[PART_OF[i], k],
                        (wide_of(1, 0, 0), tq),
                    ).start()

    def finish(k, low, many, part_id):
        part = half_v.at[k, pl.ds(1, 3), pl.ds(low, many)]
        pltpu.make_async_copy(part, part, hrecv_sem.at[part_id, k]).wait()
        part = half_v.at[k, 0, pl.ds(low, many)]
        pltpu.make_async_copy(part, part, near_sem.at[part_id, k]).wait()
        tn = (((0,), (0,)), ((), ()))
        for far in range(2):
            for i in range(low, low + many):
                both = half_v[k, 2 * far, i].astype(F32) + half_v[k, 2 * far + 1, i].astype(F32)
                same_v[k, far * 7 + i] = lax.dot_general(
                    pack, both.astype(BF), tn, preferred_element_type=F32
                ).astype(BF)
        for far in range(2):
            for a in range(4):
                n = wide_of(0, 8 - a - k, 4 - a)
                blocks = pl.ds(far * 7 + low, many)
                src = same_v.at[k, blocks, pl.ds(a * 32, 32)]
                dst = back_v.at[k * 4 + a, blocks]

                def away():
                    remote(src, dst, ysend_sem.at[k], yrecv_sem.at[k], (n, t)).start()

                if a > 0:
                    away()
                else:
                    @pl.when(k == 0)
                    def _():
                        pltpu.make_async_copy(src, dst, ysend_sem.at[k]).start()

                    pl.when(k > 0)(away)

    def expert_step(k, carry):
        @pl.when(k < 4)
        def _():
            gate_and_up(k)

        @pl.when(k < 2)
        def _():
            send_tokens(k + 2)

        @pl.when(k < 4)
        def _():
            down(k)

        @pl.when(k == 0)
        def _():
            part = q_v.at[pl.ds(1, 31)]
            pltpu.make_async_copy(part, part, qrecv_sem).wait()
            part = new_v.at[pl.ds(1, 31)]
            pltpu.make_async_copy(part, part, nrecv_sem).wait()

        @pl.when(k > 0)
        def _():
            part = same_v.at[k - 1, :, pl.ds(0, 96)]
            pltpu.make_async_copy(part, part, dsend_sem.at[k - 1]).wait()
            finish(k - 1, 0, 2, 0)
            finish(k - 1, 2, 2, 1)
            finish(k - 1, 4, 2, 2)
            finish(k - 1, 6, 1, 3)

        @pl.when(k < 4)
        def _():
            lax.fori_loop(k * 8, k * 8 + 8, attend, 0)

        return carry

    lax.fori_loop(0, 5, expert_step, 0)

    acc_v[...] = jnp.zeros_like(acc_v)

    def mix(k, carry):
        part = same_v.at[k]
        pltpu.make_async_copy(part, part, ysend_sem.at[k]).wait()

        @pl.when(k == 0)
        def _():
            part = back_v.at[pl.ds(1, 3)]
            pltpu.make_async_copy(part, part, yrecv_sem.at[k]).wait()

        @pl.when(k > 0)
        def _():
            part = back_v.at[pl.ds(k * 4, 4)]
            pltpu.make_async_copy(part, part, yrecv_sem.at[k]).wait()

        parts = []
        for far in range(2):
            for a in range(4):
                e = wide_of(far, a + k, a)
                parts.append(jnp.where(row_id == dest_v[pl.ds(e, 1), :], mixw_v[pl.ds(e, 1), :], 0.0))
        weights = jnp.concatenate(parts, axis=0)
        high = weights.astype(BF)
        low = (weights - high.astype(F32)).astype(BF)
        tn = (((0,), (0,)), ((), ()))
        for i in range(7):
            rows = jnp.concatenate([back_v[k * 4 + a, far * 7 + i] for far in range(2) for a in range(4)], axis=0)
            acc_v[:, i * 256 : (i + 1) * 256] += lax.dot_general(
                high, rows, tn, preferred_element_type=F32
            ) + lax.dot_general(low, rows, tn, preferred_element_type=F32)
        return carry

    lax.fori_loop(0, 4, mix, 0)
    moe_out[...] = acc_v[...].astype(BF)

    part = q_v.at[pl.ds(1, 31)]
    pltpu.make_async_copy(part, part, qsend_sem).wait()
    part = new_v.at[pl.ds(1, 31)]
    pltpu.make_async_copy(part, part, nsend_sem).wait()
    part = ctx_v.at[pl.ds(1, 31)]
    pltpu.make_async_copy(part, part, csend_sem).wait()
    pltpu.make_async_copy(part, part, crecv_sem).wait()
    pltpu.make_async_copy(ctx_v.at[0], attn_out.at[w], self_sem).wait()
    part = near_v.at[pl.ds(1, 3)]
    pltpu.make_async_copy(part, part, tsend_sem).wait()
    part = tok_v.at[pl.ds(96, 288)]
    pltpu.make_async_copy(part, part, gsend_sem).wait()
    pltpu.make_async_copy(other_v, other_v, dsend_sem.at[4]).wait()
    for k in range(2, 4):
        swap_sums(k).wait_send()
    for k in range(4):
        @pl.when(c == 0)
        def _():
            part = half_v.at[k, pl.ds(0, 3)]
            pltpu.make_async_copy(part, part, psend_sem.at[k]).wait()

        @pl.when(c == 1)
        def _():
            part = half_v.at[k]
            pltpu.make_async_copy(part, part, psend_sem.at[k]).wait()


def shards(
    cache, queries, new_latent, cache_len, owner, moe_tokens, expert_ids, gate_weights, w_gate, w_up, w_down
):
    ids = expert_ids.transpose(0, 2, 1)
    gates = gate_weights.transpose(0, 2, 1)

    hbm = pl.BlockSpec(memory_space=pl.ANY)
    vmem = pl.BlockSpec(memory_space=pltpu.VMEM)
    smem = pl.BlockSpec(memory_space=pltpu.SMEM)
    dma = pltpu.SemaphoreType.DMA
    attn, moe = pl.pallas_call(
        kernel,
        out_shape=(
            jax.ShapeDtypeStruct((32, 48, 512), BF),
            jax.ShapeDtypeStruct((96, QUART), BF),
        ),
        in_specs=[hbm, hbm, hbm, hbm, vmem, vmem, smem, smem, hbm, hbm, hbm],
        out_specs=(hbm, vmem),
        scratch_shapes=[
            pltpu.VMEM((32, 576, 256), BF),
            pltpu.VMEM((32, 48, 576), BF),
            pltpu.VMEM((32, 16, 128), BF),
            pltpu.VMEM((32, 48, 512), BF),
            pltpu.VMEM((384, HALF), BF),
            pltpu.VMEM((32, 96), F32),
            pltpu.VMEM((32, 96), F32),
            pltpu.VMEM((4, 32, 96), F32),
            pltpu.VMEM((32, 384), F32),
            pltpu.VMEM((3, 32, 576), BF),
            pltpu.VMEM((32, 16, 128), BF),
            pltpu.VMEM((4, 14, 128, 256), BF),
            pltpu.VMEM((4, 14, 128, 256), BF),
            pltpu.VMEM((4, 14, 256, 256), BF),
            pltpu.VMEM((2, HALF, 256), BF),
            pltpu.VMEM((2, HALF, 256), BF),
            pltpu.VMEM((512, 7168), BF),
            pltpu.VMEM((2, 256, 1024), F32),
            pltpu.VMEM((4, 128, 1024), F32),
            pltpu.VMEM((4, 4, 7, PACK, 256), BF),
            pltpu.VMEM((16, 14, 32, 256), BF),
            pltpu.VMEM((96, QUART), F32),
            dma((4,)), dma((3,)), dma((3,)), dma((3,)), dma, dma, dma, dma,
            dma, dma, dma, dma, dma, dma, dma((5,)), dma((4,)), dma((2,)), dma((4,)), dma((4,)), dma((4, 4)), dma((4, 4)),
            dma((4,)), dma((4,)), dma,
        ],
        compiler_params=pltpu.CompilerParams(
            collective_id=0, has_side_effects=True, vmem_limit_bytes=64 * 1024 * 1024 - 65536
        ),
        cost_estimate=pl.CostEstimate(flops=13_000_000_000, bytes_accessed=60_000_000, transcendentals=2_000_000),
        name="handover_attend_experts",
    )(
        queries[0].reshape(32, 48, 576), new_latent[0].transpose(1, 0, 2), cache.transpose(0, 2, 1), moe_tokens.reshape(96, 7168), ids, gates, owner, cache_len,
        w_gate[0], w_up[0], w_down[0],
    )
    return attn.reshape(1, 32, 3, 16, 512), moe.reshape(3, 32, QUART)


def solution(mesh):
    in_specs = (
        P("wide", None, None),
        P("wide", None, None, "tp", None),
        P("wide", None, None, None),
        P(),
        P(),
        P(None, "wide", None),
        P(None, "wide", None),
        P(None, "wide", None),
        P("wide", None, "tp"),
        P("wide", None, "tp"),
        P("wide", "tp", None),
    )
    out_specs = (P("wide", None, None, "tp", None), P(None, "wide", "tp"))
    return jax.shard_map(shards, mesh=mesh, in_specs=in_specs, out_specs=out_specs, check_vma=False)
```

```python
import jax
import jax.numpy as jnp
from jax import lax
from jax.experimental import pallas as pl
from jax.experimental.pallas import tpu as pltpu
from jax.sharding import PartitionSpec as P

MESH = pl.DeviceIdType.MESH
BF = jnp.bfloat16
F32 = jnp.float32
SCALE = 192.0 ** (-0.5)
MASKED = -1e30
HALF = 3584
QUART = 1792
CAP = 9
ROWS = 27
PACK = 112
PART_OF = (0, 0, 1, 1, 2, 2, 3)


def offsets(j):
    a, b, far = j % 4, (j // 4) % 4, j // 16
    return (a + b + far) % 2, (a + b) % 4, a


def kernel(
    q_hbm, new_hbm, cache_hbm, tok_hbm, ids_ref, gate_ref, owner_ref, length_ref, wg_hbm, wu_hbm, wd_hbm,
    attn_out, moe_out,
    cache_v, q_v, new_v, ctx_v, tok_v, dest_v, mixw_v, near_v, picks_v, newin_v, newout_v,
    same_v, other_v, x_v, wg_v, wu_v, wd_v, s_v, sib_v, half_v, back_v, acc_v,
    load_sem, wload_sem, wsend_sem, wrecv_sem, qsend_sem, qrecv_sem, nsend_sem, nrecv_sem,
    csend_sem, crecv_sem, gsend_sem, grecv_sem, tsend_sem, trecv_sem, dsend_sem, drecv_sem, ssend_sem, srecv_sem, psend_sem, hrecv_sem, near_sem,
    ysend_sem, yrecv_sem, self_sem,
):
    w = lax.axis_index("wide")
    t = lax.axis_index("tp")
    xl, z, y = w // 16, (w // 4) % 4, w % 4
    h, c = t // 2, t % 2
    sibling = (w, h * 2 + 1 - c)

    def wide_of(far, zz, yy):
        return ((xl + far) % 2) * 16 + ((z + zz) % 4) * 4 + (y + yy) % 4

    mine = pl.ds(pl.multiple_of(c * HALF, 128), HALF)
    theirs = pl.ds(pl.multiple_of((1 - c) * HALF, 128), HALF)
    loads = [
        pltpu.make_async_copy(tok_hbm.at[:, mine], tok_v.at[pl.ds(0, 96)], load_sem.at[0]),
        pltpu.make_async_copy(cache_hbm, cache_v, load_sem.at[1]),
        pltpu.make_async_copy(q_hbm.at[w], q_v.at[0], load_sem.at[2]),
        pltpu.make_async_copy(new_hbm, newin_v, load_sem.at[3]),
    ]
    for load in loads:
        load.start()
    hidden_rows = pl.ds(pl.multiple_of(c * 256, 256), 256)
    wloads = [
        pltpu.make_async_copy(wg_hbm.at[mine], wg_v.at[c], wload_sem.at[0]),
        pltpu.make_async_copy(wu_hbm.at[mine], wu_v.at[c], wload_sem.at[1]),
        pltpu.make_async_copy(wd_hbm, wd_v.at[hidden_rows], wload_sem.at[2]),
    ]
    for load in wloads:
        load.start()

    barrier = pltpu.get_barrier_semaphore()

    def greet(n, tq):
        pl.semaphore_signal(barrier, inc=1, device_id=(n, tq), device_id_type=MESH)

    def greet_wide(i, carry):
        greet((w + i) % 32, t)
        return carry

    lax.fori_loop(1, 32, greet_wide, 0)
    for i in range(4):
        greet(wide_of(1, i, 0), (1 - h) * 2 + c)
    for i in range(1, 4):
        greet(wide_of(1, 0, i), (1 - h) * 2 + c)
        greet(w, (t + i) % 4)
    for i in range(2):
        greet(wide_of(1, 0, 0), i * 2 + 1 - c)

    expert = lax.broadcasted_iota(jnp.int32, (32, 96), 0)
    token = lax.broadcasted_iota(jnp.int32, (32, 96), 1)
    hits = jnp.zeros((32, 96), F32)
    mixw = jnp.zeros((32, 96), F32)
    ids = jnp.concatenate([ids_ref[i] for i in range(3)], axis=1)
    gates = jnp.concatenate([gate_ref[i] for i in range(3)], axis=1)
    for k in range(8):
        equal = expert == ids[k : k + 1, :]
        hits = jnp.where(equal, 1.0, hits)
        mixw = jnp.where(equal, gates[k : k + 1, :], mixw)
    first = lax.broadcasted_iota(jnp.int32, (96, 96), 0)
    later = lax.broadcasted_iota(jnp.int32, (96, 96), 1)
    before = ((first // 32 == later // 32) & (first < later)).astype(F32)
    rank = jnp.dot(hits, before, preferred_element_type=F32)
    place = (token // 32).astype(F32) * CAP + rank
    dest_v[...] = jnp.where(hits > 0.0, place, -1.0)
    near_v[0] = dest_v[...]
    mixw_v[...] = mixw
    row_id = lax.broadcasted_iota(jnp.int32, (32, 96), 0).astype(F32)

    packed_id = lax.broadcasted_iota(jnp.int32, (PACK, 128), 0)
    padded_id = lax.broadcasted_iota(jnp.int32, (PACK, 128), 1)
    pack = (packed_id == (padded_id // 32) * ROWS + padded_id % 32) & (padded_id % 32 < ROWS)
    pack = jnp.where(pack, 1.0, 0.0).astype(BF)

    loads[3].wait()
    pieces = []
    for i in range(3):
        for j in range(5):
            piece = newin_v[i, :, j * 128 : min(j * 128 + 128, 576)]
            if j == 4:
                piece = jnp.concatenate([piece, jnp.zeros((32, 64), BF)], axis=1)
            pieces.append(piece)
    to_row = lax.broadcasted_iota(jnp.int32, (512, 480), 0)
    from_row = lax.broadcasted_iota(jnp.int32, (512, 480), 1)
    moved = (to_row // 16 == from_row % 32) & (to_row % 16 == from_row // 32)
    rows = jnp.dot(
        jnp.where(moved, 1.0, 0.0).astype(BF), jnp.concatenate(pieces, axis=0), preferred_element_type=F32
    ).astype(BF)
    for i in range(32):
        newout_v[i] = rows[i * 16 : i * 16 + 16]
    new_v[0] = newout_v[w]

    pl.semaphore_wait(barrier, 43)

    def remote(src, dst, send, recv, dev):
        return pltpu.make_async_remote_copy(
            src_ref=src, dst_ref=dst, send_sem=send, recv_sem=recv, device_id=dev, device_id_type=MESH
        )

    for d in range(1, 4):
        peer = (wide_of(0, (1 - c) * d, c * d), t)
        remote(near_v.at[0], near_v.at[d], tsend_sem, trecv_sem, peer).start()
    for part in range(4):
        for d in range(1, 4):
            peer = (wide_of(0, (1 - c) * d, c * d), t)
            cols = pl.ds(part * 896, 896)
            remote(
                tok_hbm.at[:, pl.ds(pl.multiple_of(c * HALF + part * 896, 128), 896)],
                tok_v.at[pl.ds(d * 96, 96), cols], gsend_sem, grecv_sem, peer,
            ).start()

    def send_tokens(k):
        def pick(far):
            parts = []
            for a in range(4):
                e = wide_of(far, c * (a + k), (1 - c) * a)
                held = (a + (1 - c) * k) % 4
                rows = lax.broadcasted_iota(jnp.int32, (32, 384), 0).astype(F32)
                group = lax.broadcasted_iota(jnp.int32, (32, 384), 1) // 96
                chosen = (rows == picks_v[pl.ds(e, 1), :]) & (group == held)
                parts.append(jnp.where(chosen, 1.0, 0.0))
            return jnp.concatenate(parts, axis=0).astype(BF)

        for far, out in ((0, same_v), (1, other_v)):
            picked = pick(far)
            for part in range(2):
                rows = jnp.dot(
                    picked, tok_v[:, part * QUART : (part + 1) * QUART], preferred_element_type=F32
                ).astype(BF)
                for i in range(7):
                    out[k, part * 7 + i] = rows[:, i * 256 : (i + 1) * 256]

        home = c * ((4 - k) % 4)
        kept = pl.ds(pl.multiple_of(home * 32, 32), 32)
        for i in range(14):
            x_v[k, i, kept, :] = same_v[k, i, kept, :]
        for piece in range(4):
            low, many = ((0, 4), (4, 4), (8, 3), (11, 3))[piece]
            far_low, far_many = ((0, 5), (5, 3), (8, 3), (11, 3))[piece]
            far_chip = t if piece < 1 else (1 - h) * 2 + c
            for a in range(4):
                src = pl.ds(a * 32, 32)
                away = pl.ds(128 + a * 32, 32)

                @pl.when(home != a)
                def _():
                    blocks = pl.ds(low, many)
                    remote(
                        same_v.at[k, blocks, src], x_v.at[k, blocks, src], dsend_sem.at[k], drecv_sem.at[k],
                        (wide_of(0, c * (a + k), (1 - c) * a), t),
                    ).start()

                blocks = pl.ds(far_low, far_many)
                remote(
                    other_v.at[k, blocks, src], x_v.at[k, blocks, away], dsend_sem.at[4], drecv_sem.at[k],
                    (wide_of(1, c * (a + k), (1 - c) * a), far_chip),
                ).start()

    swaps = [
        remote(wg_hbm.at[theirs], wg_v.at[c], wsend_sem.at[0], wrecv_sem.at[0], sibling),
        remote(wu_hbm.at[theirs], wu_v.at[c], wsend_sem.at[1], wrecv_sem.at[1], sibling),
        remote(wd_hbm, wd_v.at[hidden_rows], wsend_sem.at[2], wrecv_sem.at[2], sibling),
    ]
    for swap in swaps:
        swap.start()

    def send_query(j, carry):
        far, zz, yy = offsets(j)
        n = wide_of(far, zz, yy)
        remote(q_hbm.at[n], q_v.at[j], qsend_sem, qrecv_sem, (n, t)).start()
        remote(newout_v.at[n], new_v.at[j], nsend_sem, nrecv_sem, (n, t)).start()
        return carry

    lax.fori_loop(1, 16, send_query, 0)
    loads[0].wait()
    part = near_v.at[pl.ds(1, 3)]
    pltpu.make_async_copy(part, part, trecv_sem).wait()
    part = tok_v.at[pl.ds(96, 288)]
    pltpu.make_async_copy(part, part, grecv_sem).wait()
    picks_v[...] = jnp.concatenate([near_v[i] for i in range(4)], axis=1)
    send_tokens(0)
    send_tokens(1)
    lax.fori_loop(16, 32, send_query, 0)

    for load in loads[1:3]:
        load.wait()
    for load in wloads:
        load.wait()
    for swap in swaps:
        swap.wait()

    def attend(j, carry):
        far, zz, yy = offsets(j)
        o = wide_of(far, 4 - zz, 4 - yy)

        def find(r, found):
            return jnp.where(owner_ref[w * 32 + r] == o, r, found)

        held = lax.fori_loop(0, 32, find, 0)
        length = length_ref[w * 32 + held]
        latents = cache_v[held]
        query = q_v[j]
        packed = new_v[j]
        r16 = lax.broadcasted_iota(jnp.int32, (16, 16), 0)
        c16 = lax.broadcasted_iota(jnp.int32, (16, 16), 1)
        pieces = [
            jnp.dot(
                jnp.where((c16 == r16 * 5 + i) & (r16 < 3), 1.0, 0.0).astype(BF), packed,
                preferred_element_type=F32,
            ).astype(BF)
            for i in range(5)
        ]
        fresh_key = jnp.concatenate(pieces[:4], axis=1)
        nt = (((1,), (1,)), ((), ()))
        scores = jnp.dot(query, latents, preferred_element_type=F32) * SCALE
        fresh = lax.dot_general(query[:, :512], fresh_key, nt, preferred_element_type=F32)
        fresh += lax.dot_general(query[:, 512:], pieces[4][:, :64], nt, preferred_element_type=F32)
        fresh = fresh * SCALE
        valid = lax.broadcasted_iota(jnp.int32, (48, 256), 1) < length
        step = lax.broadcasted_iota(jnp.int32, (48, 16), 0) // 16
        fresh_valid = lax.broadcasted_iota(jnp.int32, (48, 16), 1) <= step
        scores = jnp.where(valid, scores, MASKED)
        fresh = jnp.where(fresh_valid, fresh, MASKED)
        top = jnp.maximum(
            jnp.max(scores, axis=1, keepdims=True), jnp.max(fresh, axis=1, keepdims=True)
        )
        weights = jnp.where(valid, jnp.exp(scores - top), 0.0)
        fresh_weights = jnp.where(fresh_valid, jnp.exp(fresh - top), 0.0)
        total = jnp.sum(weights, axis=1, keepdims=True) + jnp.sum(fresh_weights, axis=1, keepdims=True)
        context = lax.dot_general(weights.astype(BF), latents[:512, :], nt, preferred_element_type=F32)
        context += jnp.dot(fresh_weights.astype(BF), fresh_key, preferred_element_type=F32)
        ctx_v[j] = (context / total).astype(BF)

        @pl.when(j == 0)
        def _():
            pltpu.make_async_copy(ctx_v.at[j], attn_out.at[w], self_sem).start()

        @pl.when(j > 0)
        def _():
            remote(ctx_v.at[j], attn_out.at[w], csend_sem, crecv_sem, (o, t)).start()

        return carry

    def swap_sums(k):
        theirs = pl.ds(pl.multiple_of((1 - c) * 128, 128), 128)
        return remote(s_v.at[k % 2, theirs], sib_v.at[k], ssend_sem.at[k % 2], srecv_sem.at[k], sibling)

    def gate_and_up(k):
        part = x_v.at[k, :, pl.ds(0, 224)]
        pltpu.make_async_copy(part, part, drecv_sem.at[k]).wait()

        @pl.when(k >= 2)
        def _():
            swap_sums(k).wait_send()

        rows = jnp.concatenate([x_v[k, i] for i in range(14)], axis=1)
        for core in range(2):
            for i, weight in enumerate((wg_v, wu_v)):
                col = core * 512 + i * 256
                s_v[k % 2, :, col : col + 256] = jnp.dot(rows, weight[core], preferred_element_type=F32)
        swap_sums(k).start()

    def down(k):
        swap_sums(k).wait_recv()
        own = pl.ds(pl.multiple_of(c * 128, 128), 128)
        hidden = []
        for core in range(2):
            col = core * 512
            gate = s_v[k % 2, own, col : col + 256] + sib_v[k, :, col : col + 256]
            up = s_v[k % 2, own, col + 256 : col + 512] + sib_v[k, :, col + 256 : col + 512]
            hidden.append((gate / (1.0 + jnp.exp(-gate)) * up).astype(BF))
        hidden = jnp.concatenate(hidden, axis=1)
        hidden = jnp.dot(pack, hidden, preferred_element_type=F32).astype(BF)
        for i in range(28):
            x_v[k, i % 14, (i // 14) * 128 : (i // 14) * 128 + PACK, :] = jnp.dot(
                hidden, wd_v[:, i * 256 : (i + 1) * 256], preferred_element_type=F32
            ).astype(BF)

        def block(tq, i):
            n = tq * 7 + i
            return x_v.at[k, n % 14, pl.ds(pl.multiple_of((n // 14) * 128, 128), PACK)]

        @pl.when(c == 0)
        def _():
            for i in range(7):
                p = PART_OF[i]
                for core in range(2):
                    tq = 2 * (1 - h) + core
                    remote(
                        block(tq, i), half_v.at[k, 1, i], psend_sem.at[k], hrecv_sem.at[p, k], (w, tq)
                    ).start()
                pltpu.make_async_copy(block(2 * h, i), half_v.at[k, 0, i], near_sem.at[p, k]).start()
                remote(
                    block(2 * h + 1, i), half_v.at[k, 0, i], psend_sem.at[k], near_sem.at[p, k], sibling
                ).start()

        @pl.when(c == 1)
        def _():
            for i in range(7):
                for tq in (0, 2, 1, 3):
                    remote(
                        block(tq, i), half_v.at[k, 2 + h, i], psend_sem.at[k], hrecv_sem.at[PART_OF[i], k],
                        (wide_of(1, 0, 0), tq),
                    ).start()

    def finish(k, low, many, part_id):
        part = half_v.at[k, pl.ds(1, 3), pl.ds(low, many)]
        pltpu.make_async_copy(part, part, hrecv_sem.at[part_id, k]).wait()
        part = half_v.at[k, 0, pl.ds(low, many)]
        pltpu.make_async_copy(part, part, near_sem.at[part_id, k]).wait()
        tn = (((0,), (0,)), ((), ()))
        for far in range(2):
            for i in range(low, low + many):
                both = half_v[k, 2 * far, i].astype(F32) + half_v[k, 2 * far + 1, i].astype(F32)
                same_v[k, far * 7 + i] = lax.dot_general(
                    pack, both.astype(BF), tn, preferred_element_type=F32
                ).astype(BF)
        for far in range(2):
            for a in range(4):
                n = wide_of(0, 8 - a - k, 4 - a)
                blocks = pl.ds(far * 7 + low, many)
                src = same_v.at[k, blocks, pl.ds(a * 32, 32)]
                dst = back_v.at[k * 4 + a, blocks]

                def away():
                    remote(src, dst, ysend_sem.at[k], yrecv_sem.at[k], (n, t)).start()

                if a > 0:
                    away()
                else:
                    @pl.when(k == 0)
                    def _():
                        pltpu.make_async_copy(src, dst, ysend_sem.at[k]).start()

                    pl.when(k > 0)(away)

    acc_v[...] = jnp.zeros_like(acc_v)

    def mix(k, carry):
        part = same_v.at[k]
        pltpu.make_async_copy(part, part, ysend_sem.at[k]).wait()

        @pl.when(k == 0)
        def _():
            part = back_v.at[pl.ds(1, 3)]
            pltpu.make_async_copy(part, part, yrecv_sem.at[k]).wait()

        @pl.when(k > 0)
        def _():
            part = back_v.at[pl.ds(k * 4, 4)]
            pltpu.make_async_copy(part, part, yrecv_sem.at[k]).wait()

        parts = []
        for far in range(2):
            for a in range(4):
                e = wide_of(far, a + k, a)
                parts.append(jnp.where(row_id == dest_v[pl.ds(e, 1), :], mixw_v[pl.ds(e, 1), :], 0.0))
        weights = jnp.concatenate(parts, axis=0)
        high = weights.astype(BF)
        low = (weights - high.astype(F32)).astype(BF)
        tn = (((0,), (0,)), ((), ()))
        for i in range(7):
            rows = jnp.concatenate([back_v[k * 4 + a, far * 7 + i] for far in range(2) for a in range(4)], axis=0)
            acc_v[:, i * 256 : (i + 1) * 256] += lax.dot_general(
                high, rows, tn, preferred_element_type=F32
            ) + lax.dot_general(low, rows, tn, preferred_element_type=F32)
        return carry

    def expert_step(k, carry):
        @pl.when(k < 4)
        def _():
            gate_and_up(k)

        @pl.when(k < 2)
        def _():
            send_tokens(k + 2)

        @pl.when(k < 4)
        def _():
            down(k)

        @pl.when(k == 0)
        def _():
            part = q_v.at[pl.ds(1, 31)]
            pltpu.make_async_copy(part, part, qrecv_sem).wait()
            part = new_v.at[pl.ds(1, 31)]
            pltpu.make_async_copy(part, part, nrecv_sem).wait()

        @pl.when(k == 4)
        def _():
            lax.fori_loop(0, 2, mix, 0)

        @pl.when(k > 0)
        def _():
            part = same_v.at[k - 1, :, pl.ds(0, 96)]
            pltpu.make_async_copy(part, part, dsend_sem.at[k - 1]).wait()
            finish(k - 1, 0, 2, 0)
            finish(k - 1, 2, 2, 1)
            finish(k - 1, 4, 2, 2)
            finish(k - 1, 6, 1, 3)

        @pl.when(k < 4)
        def _():
            lax.fori_loop(k * 8, k * 8 + 8, attend, 0)

        return carry

    lax.fori_loop(0, 5, expert_step, 0)

    lax.fori_loop(2, 4, mix, 0)
    moe_out[...] = acc_v[...].astype(BF)

    part = q_v.at[pl.ds(1, 31)]
    pltpu.make_async_copy(part, part, qsend_sem).wait()
    part = new_v.at[pl.ds(1, 31)]
    pltpu.make_async_copy(part, part, nsend_sem).wait()
    part = ctx_v.at[pl.ds(1, 31)]
    pltpu.make_async_copy(part, part, csend_sem).wait()
    pltpu.make_async_copy(part, part, crecv_sem).wait()
    pltpu.make_async_copy(ctx_v.at[0], attn_out.at[w], self_sem).wait()
    part = near_v.at[pl.ds(1, 3)]
    pltpu.make_async_copy(part, part, tsend_sem).wait()
    part = tok_v.at[pl.ds(96, 288)]
    pltpu.make_async_copy(part, part, gsend_sem).wait()
    pltpu.make_async_copy(other_v, other_v, dsend_sem.at[4]).wait()
    for k in range(2, 4):
        swap_sums(k).wait_send()
    for k in range(4):
        @pl.when(c == 0)
        def _():
            part = half_v.at[k, pl.ds(0, 3)]
            pltpu.make_async_copy(part, part, psend_sem.at[k]).wait()

        @pl.when(c == 1)
        def _():
            part = half_v.at[k]
            pltpu.make_async_copy(part, part, psend_sem.at[k]).wait()


def shards(
    cache, queries, new_latent, cache_len, owner, moe_tokens, expert_ids, gate_weights, w_gate, w_up, w_down
):
    ids = expert_ids.transpose(0, 2, 1)
    gates = gate_weights.transpose(0, 2, 1)

    hbm = pl.BlockSpec(memory_space=pl.ANY)
    vmem = pl.BlockSpec(memory_space=pltpu.VMEM)
    smem = pl.BlockSpec(memory_space=pltpu.SMEM)
    dma = pltpu.SemaphoreType.DMA
    attn, moe = pl.pallas_call(
        kernel,
        out_shape=(
            jax.ShapeDtypeStruct((32, 48, 512), BF),
            jax.ShapeDtypeStruct((96, QUART), BF),
        ),
        in_specs=[hbm, hbm, hbm, hbm, vmem, vmem, smem, smem, hbm, hbm, hbm],
        out_specs=(hbm, vmem),
        scratch_shapes=[
            pltpu.VMEM((32, 576, 256), BF),
            pltpu.VMEM((32, 48, 576), BF),
            pltpu.VMEM((32, 16, 128), BF),
            pltpu.VMEM((32, 48, 512), BF),
            pltpu.VMEM((384, HALF), BF),
            pltpu.VMEM((32, 96), F32),
            pltpu.VMEM((32, 96), F32),
            pltpu.VMEM((4, 32, 96), F32),
            pltpu.VMEM((32, 384), F32),
            pltpu.VMEM((3, 32, 576), BF),
            pltpu.VMEM((32, 16, 128), BF),
            pltpu.VMEM((4, 14, 128, 256), BF),
            pltpu.VMEM((4, 14, 128, 256), BF),
            pltpu.VMEM((4, 14, 256, 256), BF),
            pltpu.VMEM((2, HALF, 256), BF),
            pltpu.VMEM((2, HALF, 256), BF),
            pltpu.VMEM((512, 7168), BF),
            pltpu.VMEM((2, 256, 1024), F32),
            pltpu.VMEM((4, 128, 1024), F32),
            pltpu.VMEM((4, 4, 7, PACK, 256), BF),
            pltpu.VMEM((16, 14, 32, 256), BF),
            pltpu.VMEM((96, QUART), F32),
            dma((4,)), dma((3,)), dma((3,)), dma((3,)), dma, dma, dma, dma,
            dma, dma, dma, dma, dma, dma, dma((5,)), dma((4,)), dma((2,)), dma((4,)), dma((4,)), dma((4, 4)), dma((4, 4)),
            dma((4,)), dma((4,)), dma,
        ],
        compiler_params=pltpu.CompilerParams(
            collective_id=0, has_side_effects=True, vmem_limit_bytes=64 * 1024 * 1024 - 65536
        ),
        cost_estimate=pl.CostEstimate(flops=13_000_000_000, bytes_accessed=60_000_000, transcendentals=2_000_000),
        name="handover_attend_experts",
    )(
        queries[0].reshape(32, 48, 576), new_latent[0].transpose(1, 0, 2), cache.transpose(0, 2, 1), moe_tokens.reshape(96, 7168), ids, gates, owner, cache_len,
        w_gate[0], w_up[0], w_down[0],
    )
    return attn.reshape(1, 32, 3, 16, 512), moe.reshape(3, 32, QUART)


def solution(mesh):
    in_specs = (
        P("wide", None, None),
        P("wide", None, None, "tp", None),
        P("wide", None, None, None),
        P(),
        P(),
        P(None, "wide", None),
        P(None, "wide", None),
        P(None, "wide", None),
        P("wide", None, "tp"),
        P("wide", None, "tp"),
        P("wide", "tp", None),
    )
    out_specs = (P("wide", None, None, "tp", None), P(None, "wide", "tp"))
    return jax.shard_map(shards, mesh=mesh, in_specs=in_specs, out_specs=out_specs, check_vma=False)
```
